32 devices in a mesh: section: 2 (over core), dp: 4 (over z), tensor: 4 (over y, x).
Axes of the slice: x: 2, y: 2, z: 4, core: 2. Of those that a mesh axis runs over, the one named last changes fastest.
Arguments:
- latents: bfloat16 [4, 12, 256, 768], P(None, 'dp', 'tensor'), may hold values from -6 to 6
- cond: bfloat16 [4, 12, 768], P(None, 'dp'), may hold values from -6 to 6
- cotangent: bfloat16 [4, 12, 256, 768], P(None, 'dp', 'tensor'), may hold values from -6 to 6
- live: int32 [4, 4], P(None, 'dp'), may hold values from 1 to 3, as said below
- w_qkv: bfloat16 [2, 768, 3, 768], P('section', 'dp', None, 'tensor'), may hold values from -0.21650635 to 0.21650635
- w_proj: bfloat16 [2, 768, 768], P('section', 'tensor', 'dp'), may hold values from -0.625 to 0.625
- w_up: bfloat16 [2, 768, 3072], P('section', 'dp', 'tensor'), may hold values from -0.21875 to 0.21875
- w_down: bfloat16 [2, 3072, 768], P('section', 'tensor', 'dp'), may hold values from -0.109375 to 0.109375
- w_ada: bfloat16 [2, 768, 4608], P('section', 'dp', 'tensor'), may hold values from -0.21650635 to 0.21650635
- bias_qv: bfloat16 [2, 2, 768], P('section', None, ('dp', 'tensor')), may hold values from -3 to 3
- bias_proj: bfloat16 [2, 768], P('section', ('dp', 'tensor')), may hold values from -3 to 3
- bias_up: bfloat16 [2, 3072], P('section', ('dp', 'tensor')), may hold values from -3 to 3
- bias_down: bfloat16 [2, 768], P('section', ('dp', 'tensor')), may hold values from -3 to 3
- bias_ada: bfloat16 [2, 4608], P('section', ('dp', 'tensor')), may hold values from -3 to 3
Outputs:
- layer_out: bfloat16 [2, 4, 12, 256, 768], P('section', None, 'dp', 'tensor')
- input_grad: bfloat16 [2, 4, 12, 256, 768], P('section', None, 'dp', 'tensor')
- cond_grad: bfloat16 [4, 12, 768], P(None, 'dp')
- grad_qkv: float32 [2, 768, 3, 768], P('section', 'dp', None, 'tensor')
- grad_proj: float32 [2, 768, 768], P('section', 'tensor', 'dp')
- grad_up: float32 [2, 768, 3072], P('section', 'dp', 'tensor')
- grad_down: float32 [2, 3072, 768], P('section', 'tensor', 'dp')
- grad_ada: float32 [2, 768, 4608], P('section', 'dp', 'tensor')
- grad_bias_qv: float32 [2, 2, 768], P('section', None, ('dp', 'tensor'))
- grad_bias_proj: float32 [2, 768], P('section', ('dp', 'tensor'))
- grad_bias_up: float32 [2, 3072], P('section', ('dp', 'tensor'))
- grad_bias_down: float32 [2, 768], P('section', ('dp', 'tensor'))
- grad_bias_ada: float32 [2, 4608], P('section', ('dp', 'tensor'))
The draws below stay inside these ranges and needn't reach their ends.
Inputs may be any that keep to these rules, and one draw needn't show every extreme that they name: live[m, d] latent slots of index d of dp in micro-batch m hold latents; in every micro-batch some index holds 3.
All inputs are finite; a program needn't handle non-finite values.
Results may differ from the reference program's by a relative error of at most 0.02.
Values may be sent and summed in bfloat16 or wider, within the bound.
No kernel may reach another device: no remote copies, remote signals or barrier semaphores. Data moves between devices by JAX's collectives and lax.ppermute only.
A program may use at most 192 MiB of HBM per device.

```python
import jax
import jax.numpy as jnp
from jax import lax

D = 768
HEADS = 12
HEAD_DIM = 64
FF = 3072
SEQ = 256
SLOTS = 3
MICRO = 4
LATENTS = 12


def draw_live(key, part):
    key = jax.random.fold_in(key, 11)
    count_key, full_key = jax.random.split(key)
    devices_dp = LATENTS // SLOTS
    counts = jax.random.randint(count_key, (MICRO, devices_dp), 1, SLOTS + 1)
    fullest = jax.random.randint(full_key, (MICRO, 1), 0, devices_dp)
    columns = lax.broadcasted_iota(jnp.int32, (MICRO, devices_dp), 1)
    return jnp.where(columns == fullest, SLOTS, counts).astype(jnp.int32)


def drawn_normal(key, shape_of, spread):
    return jnp.clip(jax.random.normal(key, shape_of, jnp.float32), -6.0, 6.0) * spread


def draw_latents(key, part):
    key = jax.random.fold_in(key, 21)
    shape_of = (MICRO, LATENTS, SEQ, D)
    return drawn_normal(key, shape_of, 1.0).astype(jnp.bfloat16)


def draw_cond(key, part):
    key = jax.random.fold_in(key, 22)
    shape_of = (MICRO, LATENTS, D)
    return drawn_normal(key, shape_of, 1.0).astype(jnp.bfloat16)


def draw_w_qkv(key, part):
    key = jax.random.fold_in(key, 23)
    shape_of = (2, D, 3, D)
    return drawn_normal(key, shape_of, D ** (-0.5)).astype(jnp.bfloat16)


def draw_w_ada(key, part):
    key = jax.random.fold_in(key, 24)
    shape_of = (2, D, 6 * D)
    return drawn_normal(key, shape_of, D ** (-0.5)).astype(jnp.bfloat16)


def raised(array, key, source, target, blocks, factor):
    def block_of(position):
        return (jnp.arange(array.shape[position]) // (array.shape[position] // blocks)).reshape((-1,) + (1,) * (array.ndim - 1 - position))

    one_side = jax.random.permutation(key, blocks)[block_of(target)]
    second = (block_of(target) + blocks // 2) % blocks
    return jnp.where((block_of(source) == one_side) | (block_of(source) == second), factor * array, array)


def level_of(key, dims, cuts, least, largest):
    def one(axis_at, blocks):
        steps = jax.random.uniform(jax.random.fold_in(jax.random.fold_in(key, 6), axis_at), (blocks,), jnp.float32, least / len(cuts), largest / len(cuts))
        return jnp.repeat(jnp.exp(steps), dims[axis_at] // blocks).reshape((-1,) + (1,) * (len(dims) - axis_at - 1))

    factor_of = one(*cuts[0])
    for cut in cuts[1:]:
        factor_of = factor_of * one(*cut)
    return factor_of


def scatter_about(key, shape, scale, most, shards=(), held_as=jnp.bfloat16):
    entries = scale * jax.random.normal(key, shape, jnp.float32)
    if shards:
        entries = entries * level_of(key, shape, shards, -0.22, 0.18)
    return jnp.clip(entries, -most, most).astype(held_as)


def bell_draw_with(own_key, extent, deviation, most, shards, heavy, dtype=jnp.bfloat16):
    drawn = deviation * jax.random.normal(own_key, extent, jnp.float32)
    if shards:
        drawn = drawn * level_of(own_key, extent, shards, -0.22, 0.18)
    return jnp.clip(raised(drawn, jax.random.fold_in(own_key, 3), *heavy), -most, most).astype(dtype)


def setup_inputs(seed: int = 0) -> dict:
    arg_keys = jax.random.split(jax.random.key(seed), 15)
    return {
        "latents": draw_latents(jax.random.fold_in(arg_keys[14], 71), 0),
        "cond": draw_cond(jax.random.fold_in(arg_keys[14], 71), 0),
        "cotangent": bell_draw_with(arg_keys[2], (MICRO, LATENTS, SEQ, D), 1.0, 6.0, ((1, 4), (2, 4)), (1, 3, 4, 2.0)),
        "live": draw_live(jax.random.fold_in(arg_keys[14], 71), 0),
        "w_qkv": draw_w_qkv(jax.random.fold_in(arg_keys[14], 71), 0),
        "w_proj": scatter_about(arg_keys[5], (2, D, D), (D // 8) ** -0.5, 0.625, ((0, 2), (1, 4), (2, 4))),
        "w_up": scatter_about(arg_keys[6], (2, D, FF), D ** -0.5, 0.21875, ((0, 2), (1, 4), (2, 4))),
        "w_down": scatter_about(arg_keys[7], (2, FF, D), FF ** -0.5, 0.109375, ((0, 2), (1, 4), (2, 4))),
        "w_ada": draw_w_ada(jax.random.fold_in(arg_keys[14], 71), 0),
        "bias_qv": scatter_about(arg_keys[9], (2, 2, D), 0.5, 3.0, ((0, 2), (2, 16))),
        "bias_proj": scatter_about(arg_keys[10], (2, D), 0.5, 3.0, ((0, 2), (1, 16))),
        "bias_up": scatter_about(arg_keys[11], (2, FF), 0.5, 3.0, ((0, 2), (1, 16))),
        "bias_down": scatter_about(arg_keys[12], (2, D), 0.5, 3.0, ((0, 2), (1, 16))),
        "bias_ada": scatter_about(arg_keys[13], (2, 6 * D), 0.5, 3.0, ((0, 2), (1, 16))),
    }


@jax.custom_vjp
def lower_half(v):
    return lax.optimization_barrier(v.astype(jnp.bfloat16)).astype(jnp.float32)

@jax.custom_vjp
def lower_half_backward(v):
    return v

def low_keep(v):
    return (lower_half(v), None)

def low_pass(kept, grad):
    return (grad,)

def back_keep(v):
    return (v, None)

def back_low(kept, grad):
    return (lower_half(grad),)
lower_half.defvjp(low_keep, low_pass)
lower_half_backward.defvjp(back_keep, back_low)

def layer_norm(features):
    centred = features - lax.optimization_barrier(jnp.mean(features, axis=-1, keepdims=True))
    spread = lax.optimization_barrier(jnp.mean(centred * centred, axis=-1, keepdims=True))
    return centred * lax.rsqrt(spread + 1e-06)

def gelu_tanh(features):
    return jax.nn.gelu(features, approximate=True)

def diffusion_layer(residual_stream, context_vector, parameters):
    w_qkv, w_proj, w_up, w_down, w_ada, bias_qv, bias_proj, bias_up, bias_down, bias_ada = parameters
    groups = residual_stream.shape[0]
    seq_len = residual_stream.shape[1]
    model_width = residual_stream.shape[2]
    highest = lax.Precision.HIGHEST
    act_cond = lower_half(jax.nn.silu(context_vector))
    modulate = lower_half_backward(jnp.dot(act_cond, w_ada, precision=highest) + bias_ada)
    blocks = [modulate[:, None, column * model_width:(column + 1) * model_width] for column in range(6)]
    shift_a, scale_a, gate_a, shift_b, scale_b, gate_b = blocks
    normed_a = lower_half(layer_norm(residual_stream) * (1.0 + scale_a) + shift_a)
    bias_pack = jnp.stack([bias_qv[0], jnp.zeros_like(bias_qv[0]), bias_qv[1]], axis=0)
    packed = jnp.einsum('gsd,dke->gske', normed_a, w_qkv, precision=highest) + bias_pack
    packed = lower_half_backward(lower_half(packed))
    queries = packed[:, :, 0].reshape(groups, seq_len, HEADS, HEAD_DIM)
    key_heads = packed[:, :, 1].reshape(groups, seq_len, HEADS, HEAD_DIM)
    values = packed[:, :, 2].reshape(groups, seq_len, HEADS, HEAD_DIM)
    scores = jnp.einsum('gqhe,gkhe->ghqk', queries, key_heads, precision=highest) * HEAD_DIM ** (-0.5)
    scores = lower_half_backward(scores)
    attn_probs = lower_half(jax.nn.softmax(scores, axis=-1))
    attended = jnp.einsum('ghqk,gkhe->gqhe', attn_probs, values, precision=highest)
    attended = lower_half_backward(lower_half(attended.reshape(groups, seq_len, model_width)))
    branch = lower_half_backward(jnp.einsum('gsd,de->gse', attended, w_proj, precision=highest) + bias_proj)
    middle = residual_stream + gate_a * branch
    normed_b = lower_half(layer_norm(middle) * (1.0 + scale_b) + shift_b)
    lifted = lower_half_backward(jnp.einsum('gsd,df->gsf', normed_b, w_up, precision=highest) + bias_up)
    hidden = lower_half(gelu_tanh(lifted))
    second = lower_half_backward(jnp.einsum('gsf,fd->gsd', hidden, w_down, precision=highest) + bias_down)
    return middle + gate_b * second

def reference(latents, cond, cotangent, live, w_qkv, w_proj, w_up, w_down, w_ada, bias_qv, bias_proj, bias_up, bias_down, bias_ada):
    groups = MICRO * (LATENTS // SLOTS)
    residual_stream = latents.astype(jnp.float32).reshape(groups, SLOTS, SEQ, D)
    context_vector = cond.astype(jnp.float32).reshape(groups, SLOTS, D)
    slot_ids = lax.broadcasted_iota(jnp.int32, (groups, SLOTS), 1)
    keep_mask = (slot_ids < live.reshape(groups, 1)).astype(jnp.float32)
    seed_grad = cotangent.astype(jnp.float32).reshape(groups, SLOTS, SEQ, D) * keep_mask[:, :, None, None]
    parameters = tuple((array_in.astype(jnp.float32) for array_in in (w_qkv, w_proj, w_up, w_down, w_ada, bias_qv, bias_proj, bias_up, bias_down, bias_ada)))
    probe_in = jnp.zeros_like(residual_stream)

    def forward(residual_stream, context_vector, probe_in, parameters):
        layer_first_half = tuple((array_in[0] for array_in in parameters))
        layer_second_half = tuple((array_in[1] for array_in in parameters))

        def one_group(carried, item_in):
            micro_group_input, micro_group_context, micro_group_probe = item_in
            forwarded_output = lower_half(diffusion_layer(micro_group_input, micro_group_context, layer_first_half))
            final_output = diffusion_layer(lower_half_backward(forwarded_output + micro_group_probe), micro_group_context, layer_second_half)
            return (carried, (forwarded_output, final_output))
        carried, results = lax.scan(jax.checkpoint(one_group), jnp.zeros((), jnp.float32), (residual_stream, context_vector, probe_in))
        return results
    outputs, pullback = jax.vjp(forward, residual_stream, context_vector, probe_in, parameters)
    grad_first, grad_context, grad_probe, grad_params = pullback((jnp.zeros_like(outputs[0]), seed_grad))
    shape_out = (MICRO, LATENTS, SEQ, D)
    layer_out = jnp.stack([outputs[0].reshape(shape_out), outputs[1].reshape(shape_out)]).astype(jnp.bfloat16)
    input_grad = jnp.stack([grad_first.reshape(shape_out), grad_probe.reshape(shape_out)]).astype(jnp.bfloat16)
    cond_grad = grad_context.reshape(MICRO, LATENTS, D).astype(jnp.bfloat16)
    return (layer_out, input_grad, cond_grad, grad_params[0], grad_params[1], grad_params[2], grad_params[3], grad_params[4], grad_params[5], grad_params[6], grad_params[7], grad_params[8], grad_params[9])
```

```python
import jax
import jax.numpy as jnp
from jax import lax
from jax.sharding import PartitionSpec as P

HEAD_DIM = 64
BF16 = jnp.bfloat16
F32 = jnp.float32


def layer_norm(features):
    centred = features - jnp.mean(features, axis=-1, keepdims=True)
    spread = jnp.mean(centred * centred, axis=-1, keepdims=True)
    return centred * lax.rsqrt(spread + 1e-06)


def gelu_tanh(features):
    return jax.nn.gelu(features, approximate=True)


def swap(shard, axis, step):
    peers = lax.axis_size(axis)
    return lax.ppermute(shard, axis, [(i, i ^ step) for i in range(peers)])


def turned(shard, axis, by):
    peers = lax.axis_size(axis)
    return lax.ppermute(shard, axis, [(i, (i + by) % peers) for i in range(peers)])


def pick(blocks, index):
    return lax.dynamic_index_in_dim(blocks, index, 0, keepdims=False)


def direct_dp():
    return lax.axis_size("dp") == 4


def gather_dp(shard):
    peers = lax.axis_size("dp")
    if not direct_dp():
        return lax.all_gather(shard, "dp", axis=0, tiled=True)
    place = lax.axis_index("dp")
    whole = jnp.zeros((peers,) + shard.shape, shard.dtype)
    for k in range(peers):
        piece = shard if k == 0 else turned(shard, "dp", k)
        whole = lax.dynamic_update_index_in_dim(whole, piece, (place - k) % peers, 0)
    return whole.reshape((peers * shard.shape[0],) + shard.shape[1:])


def scatter_dp(whole):
    peers = lax.axis_size("dp")
    if not direct_dp():
        return lax.psum_scatter(whole, "dp", scatter_dimension=0, tiled=True).astype(F32)
    place = lax.axis_index("dp")
    blocks = whole.reshape((peers, whole.shape[0] // peers) + whole.shape[1:])
    total = pick(blocks, place).astype(F32)
    for k in range(1, peers):
        total = total + turned(pick(blocks, (place + k) % peers), "dp", k).astype(F32)
    return total


def send_dp(blocks):
    peers = lax.axis_size("dp")
    if not direct_dp():
        return lax.all_to_all(blocks, "dp", 0, 0)
    place = lax.axis_index("dp")
    return jnp.stack(
        [pick(blocks, place)]
        + [turned(pick(blocks, (place + k) % peers), "dp", k) for k in range(1, peers)]
    )


def share_dp(shard):
    peers = lax.axis_size("dp")
    if not direct_dp():
        return lax.all_gather(shard, "dp")
    return jnp.stack([shard] + [turned(shard, "dp", k) for k in range(1, peers)])


def return_dp(blocks):
    peers = lax.axis_size("dp")
    if not direct_dp():
        return lax.all_to_all(blocks, "dp", 0, 0)
    place = lax.axis_index("dp")
    arrived = jnp.stack([blocks[0]] + [turned(blocks[k], "dp", -k) for k in range(1, peers)])
    return jnp.stack([pick(arrived, (a - place) % peers) for a in range(peers)])


def ordered(blocks):
    own = lax.axis_index("tensor")
    return jnp.stack([pick(blocks, b ^ own) for b in range(blocks.shape[0])])


def send_tensor(blocks):
    own = lax.axis_index("tensor")
    return [pick(blocks, own)] + [
        swap(pick(blocks, own ^ j), "tensor", j) for j in range(1, lax.axis_size("tensor"))
    ]


def spread_tensor(own, first, second):
    near = swap(own, "tensor", first)
    side = swap(own, "tensor", second)
    far = swap(near, "tensor", second)
    pieces = {0: own, first: near, second: side, first ^ second: far}
    return [pieces[j] for j in range(4)]


def collect_tensor(pieces, first, second):
    near = swap(pieces[first], "tensor", first)
    far = swap(pieces[first ^ second], "tensor", first)
    keep = pieces[0].astype(F32) + near.astype(F32)
    onward = (pieces[second].astype(F32) + far.astype(F32)).astype(BF16)
    return (keep + swap(onward, "tensor", second).astype(F32)).astype(BF16)


def dot(lhs, rhs, spec):
    return jnp.einsum(spec, lhs, rhs, preferred_element_type=F32)


def split_mod(modulate, width):
    return [modulate[:, None, i * width : (i + 1) * width] for i in range(6)]


def heads_of(packed):
    latents, tokens, width = packed.shape
    parts = packed.reshape(latents, tokens, 3, width // (3 * HEAD_DIM), HEAD_DIM)
    return parts[:, :, 0], parts[:, :, 1], parts[:, :, 2]


def layer_forward(incoming, modulate, weights, biases):
    w_pack, w_projt, w_up, w_downt = weights
    b_pack, b_proj, b_up, b_down = biases
    latents, tokens, width = incoming.shape
    shift_a, scale_a, gate_a, shift_b, scale_b, gate_b = split_mod(modulate, width)
    residual = incoming.astype(F32)
    normed_a = (layer_norm(residual) * (1.0 + scale_a) + shift_a).astype(BF16)
    packed = (dot(normed_a, w_pack, "gsd,dn->gsn") + b_pack).astype(BF16)
    queries, keys, values = heads_of(packed)
    scores = dot(queries, keys, "gqhe,gkhe->ghqk") * HEAD_DIM**-0.5
    top = jnp.max(scores, axis=-1, keepdims=True)
    raised = jnp.exp(scores - top)
    total = jnp.sum(raised, axis=-1, keepdims=True)
    probs = (raised / total).astype(BF16)
    log_total = top + jnp.log(total)
    attended = dot(probs, values, "ghqk,gkhe->gqhe").reshape(latents, tokens, width).astype(BF16)
    branch = dot(attended, w_projt, "gse,ne->gsn") + b_proj
    middle = residual + gate_a * branch
    normed_b = (layer_norm(middle) * (1.0 + scale_b) + shift_b).astype(BF16)
    lifted = dot(normed_b, w_up, "gsd,df->gsf") + b_up
    hidden = gelu_tanh(lifted).astype(BF16)
    second = dot(hidden, w_downt, "gsf,nf->gsn") + b_down
    output = (middle + gate_b * second).astype(BF16)
    saved = (
        normed_a,
        packed,
        log_total,
        attended,
        branch.astype(BF16),
        middle,
        normed_b,
        lifted.astype(BF16),
        hidden,
        second.astype(BF16),
    )
    return output, saved


def layer_backward(grad_out, incoming, modulate, weights, saved):
    w_pack, w_projt, w_up, w_downt = weights
    normed_a, packed, log_total, attended, branch, middle, normed_b, lifted, hidden, second = saved
    latents, tokens, width = incoming.shape
    shift_a, scale_a, gate_a, shift_b, scale_b, gate_b = split_mod(modulate, width)
    residual = incoming.astype(F32)
    grad_gate_b = jnp.sum(grad_out * second.astype(F32), axis=1)
    grad_second = (gate_b * grad_out).astype(BF16)
    grad_hidden = dot(grad_second, w_downt, "gsn,nf->gsf")
    gelu_back = jax.vjp(gelu_tanh, lifted.astype(F32))[1]
    grad_lifted = gelu_back(grad_hidden)[0].astype(BF16)
    grad_normed_b = dot(grad_lifted, w_up, "gsf,df->gsd")
    grad_shift_b = jnp.sum(grad_normed_b, axis=1)
    unit_b, norm_back_b = jax.vjp(layer_norm, middle)
    grad_scale_b = jnp.sum(grad_normed_b * unit_b, axis=1)
    grad_middle = grad_out + norm_back_b(grad_normed_b * (1.0 + scale_b))[0]
    grad_gate_a = jnp.sum(grad_middle * branch.astype(F32), axis=1)
    grad_branch = (gate_a * grad_middle).astype(BF16)
    grad_attended = dot(grad_branch, w_projt, "gsn,ne->gse").astype(BF16)
    grad_heads = grad_attended.reshape(latents, tokens, width // HEAD_DIM, HEAD_DIM)
    queries, keys, values = heads_of(packed)
    scores = dot(queries, keys, "gqhe,gkhe->ghqk") * HEAD_DIM**-0.5
    probs_exact = jnp.exp(scores - log_total)
    probs = probs_exact.astype(BF16)
    grad_values = dot(probs, grad_heads, "ghqk,gqhe->gkhe")
    grad_probs = dot(grad_heads, values, "gqhe,gkhe->ghqk")
    row_total = jnp.sum(grad_probs * probs_exact, axis=-1, keepdims=True)
    grad_scores = (probs_exact * (grad_probs - row_total)).astype(BF16)
    grad_queries = dot(grad_scores, keys, "ghqk,gkhe->gqhe") * HEAD_DIM**-0.5
    grad_keys = dot(grad_scores, queries, "ghqk,gqhe->gkhe") * HEAD_DIM**-0.5
    grad_packed = jnp.stack([grad_queries, grad_keys, grad_values], axis=2)
    grad_packed = grad_packed.reshape(latents, tokens, 3 * width).astype(BF16)
    grad_normed_a = dot(grad_packed, w_pack, "gsn,dn->gsd")
    grad_shift_a = jnp.sum(grad_normed_a, axis=1)
    unit_a, norm_back_a = jax.vjp(layer_norm, residual)
    grad_scale_a = jnp.sum(grad_normed_a * unit_a, axis=1)
    grad_input = grad_middle + norm_back_a(grad_normed_a * (1.0 + scale_a))[0]
    grad_mod = jnp.concatenate(
        [grad_shift_a, grad_scale_a, grad_gate_a, grad_shift_b, grad_scale_b, grad_gate_b], axis=-1
    ).astype(BF16)
    slabs = (
        dot(normed_a, grad_packed, "gsd,gsn->dn").astype(BF16),
        dot(grad_branch, attended, "gsn,gse->ne").astype(BF16),
        dot(normed_b, grad_lifted, "gsd,gsf->df").astype(BF16),
        dot(grad_second, hidden, "gsn,gsf->nf").astype(BF16),
    )
    bias_sums = tuple(
        jnp.sum(part.astype(F32), axis=(0, 1))
        for part in (grad_packed, grad_branch, grad_lifted, grad_second)
    )
    return grad_input.astype(BF16), grad_mod, slabs, bias_sums


def zeros_like_shapes(shapes):
    return jax.tree.map(lambda s: jnp.zeros(s.shape, s.dtype), shapes)


def body(
    latents,
    cond,
    cotangent,
    live,
    w_qkv,
    w_proj,
    w_up,
    w_down,
    w_ada,
    bias_qv,
    bias_proj,
    bias_up,
    bias_down,
    bias_ada,
):
    micros, slots, tokens_own, width = latents.shape
    ways = lax.axis_size("tensor")
    dps = lax.axis_size("dp")
    share = micros * slots // ways
    own_t = lax.axis_index("tensor")
    is_first = lax.axis_index("section") == 0
    qkv_cols = w_qkv.shape[3]
    hidden_cols = w_up.shape[2]
    mod_cols = w_ada.shape[2]
    mod_w = w_ada[0]

    pack_shard = jnp.concatenate(
        [w_qkv[0, :, 0], w_qkv[0, :, 1], w_qkv[0, :, 2], w_proj[0].T], axis=1
    )
    pack_own = gather_dp(pack_shard)
    up_own = gather_dp(w_up[0])
    down_own = gather_dp(w_down[0].T)
    qk_parts = spread_tensor(pack_own[:, : 2 * qkv_cols], 1, 2)
    vp_parts = spread_tensor(pack_own[:, 2 * qkv_cols :], 2, 1)
    up_parts = spread_tensor(up_own, 1, 2)
    down_parts = spread_tensor(down_own, 2, 1)

    source = jnp.where(is_first, latents, cotangent).reshape(ways, share, tokens_own, width)
    tokens_in = jnp.concatenate(send_tensor(source), axis=1)

    bias_shard = jnp.concatenate(
        [bias_qv[0, 0], bias_qv[0, 1], bias_proj[0], bias_up[0], bias_down[0], bias_ada[0]]
    )
    cuts = [bias_qv.shape[2]] * 2 + [b.shape[1] for b in (bias_proj, bias_up, bias_down, bias_ada)]
    bias_dp = gather_dp(bias_shard[None])
    bias_rel = jnp.stack(
        [bias_dp] + [swap(bias_dp, "tensor", j) for j in range(1, ways)]
    )
    bias_all = jnp.transpose(ordered(bias_rel), (1, 0, 2)).astype(F32)
    full, start = [], 0
    for cut in cuts:
        full.append(bias_all[:, :, start : start + cut].reshape(-1))
        start += cut
    full_q, full_v, full_proj, full_up, full_down, full_ada = full
    by_xor = lambda vector: ordered(vector.reshape(ways, -1)).reshape(-1)
    bias_pack = jnp.concatenate([by_xor(full_q), jnp.zeros_like(full_q), by_xor(full_v)])
    biases = (bias_pack, full_proj, by_xor(full_up), full_down)

    context = cond.reshape(micros * slots, width)
    act = jax.nn.silu(context.astype(F32)).astype(BF16)
    act_blocks = jnp.transpose(act.reshape(micros * slots, dps, width // dps), (1, 0, 2))
    act_all = send_dp(act_blocks)
    mod_terms = return_dp(dot(act_all, mod_w, "kgd,dm->kgm"))
    bias_mod = lax.dynamic_slice_in_dim(full_ada, own_t * mod_cols, mod_cols)
    mod_block = jnp.sum(mod_terms, axis=0) + bias_mod
    mod_rel = jnp.stack(send_tensor(mod_block.reshape(ways, share, mod_cols)))
    modulate = jnp.transpose(ordered(mod_rel), (1, 0, 2)).reshape(share, ways * mod_cols)

    weights = (
        jnp.concatenate(
            [part[:, :qkv_cols] for part in qk_parts]
            + [part[:, qkv_cols:] for part in qk_parts]
            + [part[:, :qkv_cols] for part in vp_parts],
            axis=1,
        ),
        jnp.concatenate([part[:, qkv_cols:] for part in vp_parts], axis=1),
        jnp.concatenate(up_parts, axis=1),
        jnp.concatenate(down_parts, axis=1),
    )

    slot_mask = (lax.broadcasted_iota(jnp.int32, (micros, slots), 1) < live).astype(F32)
    own_mask = pick(slot_mask.reshape(ways, share), own_t)

    def first_forward(args):
        tokens, modulate, weights, biases = args
        return layer_forward(tokens, modulate, weights, biases)

    args = (tokens_in, modulate, weights, biases)
    shapes = jax.eval_shape(first_forward, args)
    output_first, saved_first = lax.cond(
        is_first, first_forward, lambda args: zeros_like_shapes(shapes), args
    )
    arrived = lax.ppermute(output_first, "section", [(0, 1)])

    def second_both(args):
        arrived, tokens, own_mask, modulate, weights, biases = args
        output, saved = layer_forward(arrived, modulate, weights, biases)
        grad_out = tokens.astype(F32) * own_mask[:, None, None]
        return output, layer_backward(grad_out, arrived, modulate, weights, saved)

    args = (arrived, tokens_in, own_mask, modulate, weights, biases)
    shapes_both = jax.eval_shape(second_both, args)
    output_second, grads_second = lax.cond(
        is_first, lambda args: zeros_like_shapes(shapes_both), second_both, args
    )
    back = lax.ppermute(grads_second[0], "section", [(1, 0)])

    def first_backward(args):
        back, tokens, modulate, weights, saved, other = args
        return layer_backward(back.astype(F32), tokens, modulate, weights, saved)

    args = (back, tokens_in, modulate, weights, saved_first, grads_second)
    grad_input, grad_mod, slabs, bias_sums = lax.cond(
        is_first, first_backward, lambda args: args[-1], args
    )
    output = jnp.where(is_first, output_first, output_second)

    g_pack, g_projt, g_up, g_downt = slabs
    third = qkv_cols * ways
    g_qk = [
        jnp.concatenate(
            [
                g_pack[:, j * qkv_cols : (j + 1) * qkv_cols],
                g_pack[:, third + j * qkv_cols : third + (j + 1) * qkv_cols],
            ],
            axis=1,
        )
        for j in range(ways)
    ]
    g_vp = [
        jnp.concatenate(
            [
                g_pack[:, 2 * third + j * qkv_cols : 2 * third + (j + 1) * qkv_cols],
                g_projt[:, j * qkv_cols : (j + 1) * qkv_cols],
            ],
            axis=1,
        )
        for j in range(ways)
    ]
    blocks = lambda whole: [
        whole[:, j * hidden_cols : (j + 1) * hidden_cols] for j in range(ways)
    ]
    out_down = scatter_dp(collect_tensor(blocks(g_downt), 2, 1))
    out_up = scatter_dp(collect_tensor(blocks(g_up), 1, 2))
    out_pack = scatter_dp(
        jnp.concatenate([collect_tensor(g_qk, 1, 2), collect_tensor(g_vp, 2, 1)], axis=1)
    )
    shard_qkv = out_pack[:, : 3 * qkv_cols].reshape(-1, 3, qkv_cols)
    shard_proj = out_pack[:, 3 * qkv_cols :].T
    shard_up = out_up
    shard_down = out_down.T

    grad_groups = jnp.transpose(grad_mod.reshape(share, ways, mod_cols), (1, 0, 2))
    grad_block = ordered(jnp.stack(send_tensor(grad_groups)))
    grad_all = share_dp(grad_block.reshape(micros * slots, mod_cols))
    shard_ada = dot(act_all, grad_all, "kgd,kgm->dm")
    ctx_terms = return_dp(dot(grad_all, mod_w, "kgm,dm->kgd").astype(BF16))
    ctx = jnp.transpose(ctx_terms, (1, 0, 2)).reshape(micros * slots, width)
    for axis, step in (("tensor", 1), ("tensor", 2), ("section", 1)):
        ctx = (ctx.astype(F32) + swap(ctx, axis, step).astype(F32)).astype(BF16)
    silu_back = jax.vjp(jax.nn.silu, cond.astype(F32))[1]
    cond_grad = silu_back(ctx.astype(F32).reshape(cond.shape))[0].astype(BF16)

    sum_pack, sum_branch, sum_lifted, sum_second = bias_sums
    parts = [
        by_xor(sum_pack[:third]),
        by_xor(sum_pack[2 * third :]),
        sum_branch,
        by_xor(sum_lifted),
        sum_second,
        jnp.sum(grad_mod.astype(F32), axis=0),
    ]
    bias_terms = jnp.concatenate([part.reshape(dps, ways, -1) for part in parts], axis=2)
    bias_terms = scatter_dp(bias_terms)[0]
    bias_out = sum(send_tensor(bias_terms))
    pieces, start = [], 0
    for cut in cuts:
        pieces.append(bias_out[start : start + cut])
        start += cut

    def handed_back(whole):
        split = jnp.transpose(whole.reshape(share, ways, tokens_own, width), (1, 0, 2, 3))
        arrivals = [split[0]] + [swap(split[j], "tensor", j) for j in range(1, ways)]
        return ordered(jnp.stack(arrivals)).reshape(latents.shape)

    layer_out = handed_back(output)
    input_grad = handed_back(grad_input)
    return (
        layer_out[None],
        input_grad[None],
        cond_grad,
        shard_qkv[None],
        shard_proj[None],
        shard_up[None],
        shard_down[None],
        shard_ada[None],
        jnp.stack(pieces[:2])[None],
        pieces[2][None],
        pieces[3][None],
        pieces[4][None],
        pieces[5][None],
    )


def solution(mesh):
    both = ("dp", "tensor")
    return jax.shard_map(
        body,
        mesh=mesh,
        in_specs=(
            P(None, "dp", "tensor", None),
            P(None, "dp", None),
            P(None, "dp", "tensor", None),
            P(None, "dp"),
            P("section", "dp", None, "tensor"),
            P("section", "tensor", "dp"),
            P("section", "dp", "tensor"),
            P("section", "tensor", "dp"),
            P("section", "dp", "tensor"),
            P("section", None, both),
            P("section", both),
            P("section", both),
            P("section", both),
            P("section", both),
        ),
        out_specs=(
            P("section", None, "dp", "tensor", None),
            P("section", None, "dp", "tensor", None),
            P(None, "dp", None),
            P("section", "dp", None, "tensor"),
            P("section", "tensor", "dp"),
            P("section", "dp", "tensor"),
            P("section", "tensor", "dp"),
            P("section", "dp", "tensor"),
            P("section", None, both),
            P("section", both),
            P("section", both),
            P("section", both),
            P("section", both),
        ),
        check_vma=False,
    )
```

```python
import functools
import math

import jax
import jax.numpy as jnp
from jax import lax
from jax.experimental import pallas as pl
from jax.experimental.pallas import tpu as pltpu
from jax.sharding import PartitionSpec as P

HEAD_DIM = 64
BF16 = jnp.bfloat16
F32 = jnp.float32


def swap(shard, axis, step):
    peers = lax.axis_size(axis)
    return lax.ppermute(shard, axis, [(i, i ^ step) for i in range(peers)])


def turned(shard, axis, by):
    peers = lax.axis_size(axis)
    return lax.ppermute(shard, axis, [(i, (i + by) % peers) for i in range(peers)])


def pick(blocks, index):
    return lax.dynamic_index_in_dim(blocks, index, 0, keepdims=False)


def direct_dp():
    return lax.axis_size("dp") == 4


def gather_dp(shard):
    peers = lax.axis_size("dp")
    if not direct_dp():
        return lax.all_gather(shard, "dp", axis=0, tiled=True)
    place = lax.axis_index("dp")
    whole = jnp.zeros((peers,) + shard.shape, shard.dtype)
    for k in range(peers):
        piece = shard if k == 0 else turned(shard, "dp", k)
        whole = lax.dynamic_update_index_in_dim(whole, piece, (place - k) % peers, 0)
    return whole.reshape((peers * shard.shape[0],) + shard.shape[1:])


def scatter_dp(whole):
    peers = lax.axis_size("dp")
    if not direct_dp():
        return lax.psum_scatter(whole, "dp", scatter_dimension=0, tiled=True).astype(F32)
    place = lax.axis_index("dp")
    blocks = whole.reshape((peers, whole.shape[0] // peers) + whole.shape[1:])
    total = pick(blocks, place).astype(F32)
    for k in range(1, peers):
        total = total + turned(pick(blocks, (place + k) % peers), "dp", k).astype(F32)
    return total


def send_dp(blocks):
    peers = lax.axis_size("dp")
    if not direct_dp():
        return lax.all_to_all(blocks, "dp", 0, 0)
    place = lax.axis_index("dp")
    return jnp.stack(
        [pick(blocks, place)]
        + [turned(pick(blocks, (place + k) % peers), "dp", k) for k in range(1, peers)]
    )


def share_dp(shard):
    peers = lax.axis_size("dp")
    if not direct_dp():
        return lax.all_gather(shard, "dp")
    return jnp.stack([shard] + [turned(shard, "dp", k) for k in range(1, peers)])


def return_dp(blocks):
    peers = lax.axis_size("dp")
    if not direct_dp():
        return lax.all_to_all(blocks, "dp", 0, 0)
    place = lax.axis_index("dp")
    arrived = jnp.stack([blocks[0]] + [turned(blocks[k], "dp", -k) for k in range(1, peers)])
    return jnp.stack([pick(arrived, (a - place) % peers) for a in range(peers)])


def ordered(blocks):
    own = lax.axis_index("tensor")
    return jnp.stack([pick(blocks, b ^ own) for b in range(blocks.shape[0])])


def send_tensor(blocks):
    own = lax.axis_index("tensor")
    return [pick(blocks, own)] + [
        swap(pick(blocks, own ^ j), "tensor", j) for j in range(1, lax.axis_size("tensor"))
    ]


def spread_tensor(own, first, second):
    near = swap(own, "tensor", first)
    side = swap(own, "tensor", second)
    far = swap(near, "tensor", second)
    pieces = {0: own, first: near, second: side, first ^ second: far}
    return [pieces[j] for j in range(4)]


def collect_tensor(pieces, first, second):
    near = swap(pieces[first], "tensor", first)
    far = swap(pieces[first ^ second], "tensor", first)
    keep = pieces[0].astype(F32) + near.astype(F32)
    onward = (pieces[second].astype(F32) + far.astype(F32)).astype(BF16)
    return (keep + swap(onward, "tensor", second).astype(F32)).astype(BF16)


VMEM_BYTES = 50 * 1024 * 1024
GELU_A = 0.7978845608028654
GELU_B = 0.044715


def dot(lhs, rhs, spec):
    return jnp.einsum(spec, lhs, rhs, preferred_element_type=F32)


def mm(lhs, rhs):
    return jnp.dot(lhs, rhs, preferred_element_type=F32)


def mm_nt(lhs, rhs):
    return lax.dot_general(lhs, rhs, (((1,), (1,)), ((), ())), preferred_element_type=F32)


def mm_tn(lhs, rhs):
    return lax.dot_general(lhs, rhs, (((0,), (0,)), ((), ())), preferred_element_type=F32)


def norm_parts(features):
    centred = features - jnp.mean(features, axis=-1, keepdims=True)
    spread = jnp.mean(centred * centred, axis=-1, keepdims=True)
    rate = lax.rsqrt(spread + 1e-06)
    return centred * rate, rate


def norm_back(unit, rate, grad):
    lean = jnp.mean(grad, axis=-1, keepdims=True)
    tilt = jnp.mean(grad * unit, axis=-1, keepdims=True)
    return rate * (grad - lean - unit * tilt)


def token_sum(part):
    return jnp.sum(part, axis=0, keepdims=True)


def head_cols(block, start, head):
    return block[:, start + head * HEAD_DIM : start + (head + 1) * HEAD_DIM]


def attend_kernel(ways, heads, refs):
    x_ref, mod_ref, bqk_ref, bv_ref, bproj_ref = refs[:5]
    qk_w, vp_w = refs[5 : 5 + ways], refs[5 + ways : 5 + 2 * ways]
    na_ref, qk_ref, v_ref, att_ref, branch_ref, middle_ref, nb_ref = refs[5 + 2 * ways :]
    cols = heads * HEAD_DIM
    scale = HEAD_DIM**-0.5
    x = x_ref[0].astype(F32)
    shift_a, scale_a, gate_a = (mod_ref[0, i : i + 1, :] for i in range(3))
    shift_b, scale_b = (mod_ref[0, i : i + 1, :] for i in (3, 4))
    normed = (norm_parts(x)[0] * (1.0 + scale_a) + shift_a).astype(BF16)
    na_ref[0] = normed
    branch = jnp.zeros_like(x) + bproj_ref[...]
    for j in range(ways):
        qk = (mm(normed, qk_w[j][...]) + bqk_ref[j : j + 1, :]).astype(BF16)
        value = (mm(normed, vp_w[j][:, :cols]) + bv_ref[j : j + 1, :]).astype(BF16)
        qk_ref[0, j] = qk
        v_ref[0, j] = value
        outs = [jnp.zeros((x.shape[0], cols), F32)]
        for h in range(heads):
            scores = mm_nt(head_cols(qk, 0, h), head_cols(qk, cols, h)) * scale
            raised = jnp.exp(scores - jnp.max(scores, axis=-1, keepdims=True))
            probs = raised / jnp.sum(raised, axis=-1, keepdims=True)
            outs.append(mm(probs.astype(BF16), head_cols(value, 0, h)))
        padded = jnp.concatenate(outs, axis=1).astype(BF16)
        att_ref[0, j] = padded
        branch = branch + mm_nt(padded, vp_w[j][...])
    branch_ref[0] = branch.astype(BF16)
    middle = x + gate_a * branch
    middle_ref[0] = middle
    nb_ref[0] = (norm_parts(middle)[0] * (1.0 + scale_b) + shift_b).astype(BF16)


def lift_kernel(pieces, refs):
    nb_ref, middle_ref, mod_ref, bup_ref, bdown_ref = refs[:5]
    up_w, down_w = refs[5 : 5 + pieces], refs[5 + pieces : 5 + 2 * pieces]
    lifted_ref, hidden_ref, second_ref, out_ref = refs[5 + 2 * pieces :]
    normed = nb_ref[0]
    middle = middle_ref[0]
    gate_b = mod_ref[0, 5:6, :]
    second = jnp.zeros_like(middle) + bdown_ref[...]
    for c in range(pieces):
        part = up_w[c].shape[1]
        lifted = mm(normed, up_w[c][...]) + bup_ref[c : c + 1, :]
        turn = jnp.tanh(GELU_A * (lifted + GELU_B * lifted * lifted * lifted))
        hidden = (0.5 * lifted * (1.0 + turn)).astype(BF16)
        lifted_ref[0, :, c * part : (c + 1) * part] = lifted.astype(BF16)
        hidden_ref[0, :, c * part : (c + 1) * part] = hidden
        second = second + mm_nt(hidden, down_w[c][...])
    second_ref[0] = second.astype(BF16)
    out_ref[0] = (middle + gate_b * second).astype(BF16)


def lift_back_kernel(pieces, refs):
    g_ref, second_ref, lifted_ref, middle_ref, mod_ref = refs[:5]
    up_w, down_w = refs[5 : 5 + pieces], refs[5 + pieces : 5 + 2 * pieces]
    gs_ref, gl_ref, gm_ref, sums_ref, lift_sums_ref = refs[5 + 2 * pieces :]
    grad = g_ref[0].astype(F32)
    scale_b, gate_b = mod_ref[0, 4:5, :], mod_ref[0, 5:6, :]
    grad_second = (gate_b * grad).astype(BF16)
    gs_ref[0] = grad_second
    normed = jnp.zeros_like(grad)
    for c in range(pieces):
        part = up_w[c].shape[1]
        grad_hidden = mm(grad_second, down_w[c][...])
        v = lifted_ref[0, :, c * part : (c + 1) * part].astype(F32)
        square = v * v
        turn = jnp.tanh(GELU_A * v * (1.0 + GELU_B * square))
        slope = 0.5 * (1.0 + turn) + (0.5 * GELU_A) * v * (1.0 - turn * turn) * (
            1.0 + (3.0 * GELU_B) * square
        )
        grad_lifted = (grad_hidden * slope).astype(BF16)
        gl_ref[0, :, c * part : (c + 1) * part] = grad_lifted
        lift_sums_ref[0, c : c + 1, :] = token_sum(grad_lifted.astype(F32))
        normed = normed + mm_nt(grad_lifted, up_w[c][...])
    unit, rate = norm_parts(middle_ref[0])
    gm_ref[0] = grad + norm_back(unit, rate, normed * (1.0 + scale_b))
    sums_ref[0, 0:1, :] = token_sum(normed)
    sums_ref[0, 1:2, :] = token_sum(normed * unit)
    sums_ref[0, 2:3, :] = token_sum(grad * second_ref[0].astype(F32))
    sums_ref[0, 3:4, :] = token_sum(grad_second.astype(F32))


def attend_back_kernel(ways, heads, refs):
    gm_ref, branch_ref, qk_ref, v_ref, x_ref, mod_ref = refs[:6]
    qk_w, vp_w = refs[6 : 6 + ways], refs[6 + ways : 6 + 2 * ways]
    gb_ref, gqk_ref, gv_ref, gi_ref, sums_ref, pack_sums_ref = refs[6 + 2 * ways :]
    cols = heads * HEAD_DIM
    scale = HEAD_DIM**-0.5
    middle = gm_ref[0]
    scale_a, gate_a = mod_ref[0, 1:2, :], mod_ref[0, 2:3, :]
    grad_branch = (gate_a * middle).astype(BF16)
    gb_ref[0] = grad_branch
    normed = jnp.zeros_like(middle)
    for j in range(ways):
        grad_att = mm(grad_branch, vp_w[j][...]).astype(BF16)
        qk = qk_ref[0, j]
        value = v_ref[0, j]
        grads_q, grads_k, grads_v = [], [], []
        for h in range(heads):
            query, key = head_cols(qk, 0, h), head_cols(qk, cols, h)
            grad_head = head_cols(grad_att, cols, h)
            scores = mm_nt(key, query) * scale
            raised = jnp.exp(scores - jnp.max(scores, axis=0, keepdims=True))
            probs = raised / jnp.sum(raised, axis=0, keepdims=True)
            grads_v.append(mm(probs.astype(BF16), grad_head))
            grad_probs = mm_nt(head_cols(value, 0, h), grad_head)
            total = jnp.sum(grad_probs * probs, axis=0, keepdims=True)
            grad_scores = (probs * (grad_probs - total)).astype(BF16)
            grads_k.append(mm(grad_scores, query) * scale)
            grads_q.append(mm_tn(grad_scores, key) * scale)
        grad_qk = jnp.concatenate(grads_q + grads_k, axis=1).astype(BF16)
        grads_v.append(jnp.zeros((middle.shape[0], cols), F32))
        grad_v = jnp.concatenate(grads_v, axis=1).astype(BF16)
        gqk_ref[0, j] = grad_qk
        gv_ref[0, j] = grad_v
        pack_sums_ref[0, j : j + 1, :] = token_sum(grad_qk.astype(F32))
        pack_sums_ref[0, ways + j : ways + j + 1, :] = token_sum(grad_v.astype(F32))
        normed = normed + mm_nt(grad_qk, qk_w[j][...]) + mm_nt(grad_v, vp_w[j][...])
    unit, rate = norm_parts(x_ref[0].astype(F32))
    gi_ref[0] = (middle + norm_back(unit, rate, normed * (1.0 + scale_a))).astype(BF16)
    sums_ref[0, 0:1, :] = token_sum(normed)
    sums_ref[0, 1:2, :] = token_sum(normed * unit)
    sums_ref[0, 2:3, :] = token_sum(middle * branch_ref[0].astype(F32))
    sums_ref[0, 3:4, :] = token_sum(grad_branch.astype(F32))


def flat_tokens(ref):
    return ref[...].reshape(ref.shape[0] * ref.shape[1], ref.shape[2])


def lift_weights_kernel(pieces, refs):
    nb_ref, gl_ref, gs_ref, hidden_ref = refs[:4]
    up_out, down_out = refs[4 : 4 + pieces], refs[4 + pieces : 4 + 2 * pieces]
    for left_ref, right_ref, outs in ((gs_ref, hidden_ref, down_out), (nb_ref, gl_ref, up_out)):
        left = flat_tokens(left_ref).T
        for c in range(pieces):
            part = outs[c].shape[1]
            right = right_ref[:, :, c * part : (c + 1) * part]
            right = right.reshape(right.shape[0] * right.shape[1], part)
            outs[c][...] = mm(left, right).astype(BF16)


def attend_weights_kernel(ways, refs):
    na_ref, gqk_ref, gv_ref, gb_ref, att_ref = refs[:5]
    qk_out, vp_out = refs[5 : 5 + ways], refs[5 + ways : 5 + 2 * ways]
    latents, tokens = na_ref.shape[:2]
    left_n = flat_tokens(na_ref).T
    left_b = flat_tokens(gb_ref).T
    for j in range(ways):
        over = lambda ref: jnp.concatenate([ref[g, j] for g in range(latents)], axis=0)
        qk_out[j][...] = mm(left_n, over(gqk_ref)).astype(BF16)
        vp_out[j][...] = (mm(left_n, over(gv_ref)) + mm(left_b, over(att_ref))).astype(BF16)


def per_latent(shape):
    rank = len(shape)
    return pl.BlockSpec((1,) + tuple(shape[1:]), lambda g: (g,) + (0,) * (rank - 1))


def constant(shape):
    rank = len(shape)
    return pl.BlockSpec(tuple(shape), lambda g: (0,) * rank, pipeline_mode=pl.Buffered(1))


def over_latents(kernel, name, varying, fixed, outs, flops):
    return pl.pallas_call(
        lambda *refs: kernel(refs),
        grid=(varying[0].shape[0],),
        in_specs=[per_latent(a.shape) for a in varying] + [constant(a.shape) for a in fixed],
        out_specs=[per_latent(shape) for shape, _ in outs],
        out_shape=[jax.ShapeDtypeStruct(shape, dtype) for shape, dtype in outs],
        compiler_params=pltpu.CompilerParams(vmem_limit_bytes=VMEM_BYTES),
        cost_estimate=pl.CostEstimate(
            flops=flops,
            bytes_accessed=sum(a.size * a.dtype.itemsize for a in varying + fixed)
            + sum(4 * math.prod(shape) for shape, _ in outs),
            transcendentals=0,
        ),
        name=name,
    )(*varying, *fixed)


def at_once(kernel, name, inputs, out_shapes, flops):
    return pl.pallas_call(
        lambda *refs: kernel(refs),
        in_specs=[pl.BlockSpec(memory_space=pltpu.VMEM)] * len(inputs),
        out_specs=[pl.BlockSpec(memory_space=pltpu.VMEM)] * len(out_shapes),
        out_shape=[jax.ShapeDtypeStruct(shape, BF16) for shape in out_shapes],
        compiler_params=pltpu.CompilerParams(vmem_limit_bytes=VMEM_BYTES),
        cost_estimate=pl.CostEstimate(
            flops=flops,
            bytes_accessed=sum(a.size * a.dtype.itemsize for a in inputs)
            + sum(2 * math.prod(shape) for shape in out_shapes),
            transcendentals=0,
        ),
        name=name,
    )(*inputs)


def attend_forward(tokens_in, mod6, weights, biases):
    qk_w, vp_w = weights[:2]
    b_qk, b_v, b_proj = biases[:3]
    ways, cols = len(qk_w), b_v.shape[1]
    latents, tokens, width = tokens_in.shape
    whole = (latents, tokens, width)
    return over_latents(
        functools.partial(attend_kernel, ways, cols // HEAD_DIM),
        "attend_forward",
        [tokens_in, mod6],
        [b_qk, b_v, b_proj, *qk_w, *vp_w],
        [
            (whole, BF16),
            ((latents, ways, tokens, 2 * cols), BF16),
            ((latents, ways, tokens, cols), BF16),
            ((latents, ways, tokens, 2 * cols), BF16),
            (whole, BF16),
            (whole, F32),
            (whole, BF16),
        ],
        10 * latents * tokens * width * width,
    )


def lift_forward(normed_b, middle, mod6, weights, biases):
    up_w, down_w = weights[2:]
    b_up, b_down = biases[3:]
    whole = middle.shape
    wide = whole[:2] + (b_up.size,)
    return over_latents(
        functools.partial(lift_kernel, len(up_w)),
        "lift_forward",
        [normed_b, middle, mod6],
        [b_up, b_down, *up_w, *down_w],
        [(wide, BF16), (wide, BF16), (whole, BF16), (whole, BF16)],
        4 * math.prod(whole) * b_up.size,
    )


def layer_forward(tokens_in, mod6, weights, biases):
    normed_a, qk, value, attended, branch, middle, normed_b = attend_forward(
        tokens_in, mod6, weights, biases
    )
    lifted, hidden, second, output = lift_forward(normed_b, middle, mod6, weights, biases)
    saved_a = (normed_a, qk, value, attended, branch)
    saved_b = (middle, normed_b, lifted, hidden, second)
    return output, saved_a, saved_b


def lift_backward(grad_out, mod6, weights, saved_b):
    up_w, down_w = weights[2:]
    middle, normed_b, lifted, hidden, second = saved_b
    latents, tokens, width = middle.shape
    grad_second, grad_lifted, grad_middle, sums, lift_sums = over_latents(
        functools.partial(lift_back_kernel, len(up_w)),
        "lift_backward",
        [grad_out, second, lifted, middle, mod6],
        [*up_w, *down_w],
        [
            (middle.shape, BF16),
            (lifted.shape, BF16),
            (middle.shape, F32),
            ((latents, 4, width), F32),
            ((latents, len(up_w), up_w[0].shape[1]), F32),
        ],
        4 * middle.size * lifted.shape[2],
    )
    return grad_middle, (normed_b, grad_lifted, grad_second, hidden), (sums, lift_sums)


def attend_backward(grad_middle, tokens_in, mod6, weights, saved_a):
    qk_w, vp_w = weights[:2]
    normed_a, qk, value, attended, branch = saved_a
    latents, tokens, width = grad_middle.shape
    cols = value.shape[3]
    grad_branch, grad_qk, grad_v, grad_input, sums, pack_sums = over_latents(
        functools.partial(attend_back_kernel, len(qk_w), cols // HEAD_DIM),
        "attend_backward",
        [grad_middle, branch, qk, value, tokens_in, mod6],
        [*qk_w, *vp_w],
        [
            (grad_middle.shape, BF16),
            (qk.shape, BF16),
            (qk.shape, BF16),
            (grad_middle.shape, BF16),
            ((latents, 4, width), F32),
            ((latents, 2 * len(qk_w), 2 * cols), F32),
        ],
        12 * grad_middle.size * width,
    )
    return grad_input, (normed_a, grad_qk, grad_v, grad_branch, attended), (sums, pack_sums)


def lift_weights(kept, pieces):
    normed_b, grad_lifted = kept[:2]
    width, wide = normed_b.shape[2], grad_lifted.shape[2]
    return at_once(
        functools.partial(lift_weights_kernel, pieces),
        "lift_weights",
        kept,
        [(width, wide // pieces)] * (2 * pieces),
        4 * normed_b.size * wide,
    )


def attend_weights(kept):
    normed_a, grad_qk = kept[:2]
    ways, part = grad_qk.shape[1], grad_qk.shape[3]
    return at_once(
        functools.partial(attend_weights_kernel, ways),
        "attend_weights",
        kept,
        [(normed_a.shape[2], part)] * (2 * ways),
        6 * normed_a.size * ways * part,
    )


def zeros_like_shapes(shapes):
    return jax.tree.map(lambda s: jnp.zeros(s.shape, s.dtype), shapes)


def after(value, *others):
    return lax.optimization_barrier((value,) + others)[0]


def body(
    latents,
    cond,
    cotangent,
    live,
    w_qkv,
    w_proj,
    w_up,
    w_down,
    w_ada,
    bias_qv,
    bias_proj,
    bias_up,
    bias_down,
    bias_ada,
):
    micros, slots, tokens_own, width = latents.shape
    ways = lax.axis_size("tensor")
    dps = lax.axis_size("dp")
    share = micros * slots // ways
    own_t = lax.axis_index("tensor")
    is_first = lax.axis_index("section") == 0
    qkv_cols = w_qkv.shape[3]
    hidden_cols = w_up.shape[2]
    mod_cols = w_ada.shape[2]
    mod_w = w_ada[0]

    source = jnp.where(is_first, latents, cotangent).reshape(ways, share, tokens_own, width)
    tokens_in = jnp.concatenate(send_tensor(source), axis=1)

    bias_shard = jnp.concatenate(
        [bias_qv[0, 0], bias_qv[0, 1], bias_proj[0], bias_up[0], bias_down[0], bias_ada[0]]
    )
    cuts = [bias_qv.shape[2]] * 2 + [b.shape[1] for b in (bias_proj, bias_up, bias_down, bias_ada)]
    bias_dp = gather_dp(bias_shard[None])
    bias_rel = jnp.stack(
        [bias_dp] + [swap(bias_dp, "tensor", j) for j in range(1, ways)]
    )
    bias_all = jnp.transpose(ordered(bias_rel), (1, 0, 2)).astype(F32)
    full, start = [], 0
    for cut in cuts:
        full.append(bias_all[:, :, start : start + cut].reshape(-1))
        start += cut
    full_q, full_v, full_proj, full_up, full_down, full_ada = full
    by_xor = lambda vector: ordered(vector.reshape(ways, -1)).reshape(-1)
    bias_qk = by_xor(full_q).reshape(ways, -1)
    bias_qk = jnp.concatenate([bias_qk, jnp.zeros_like(bias_qk)], axis=1)
    biases = (
        bias_qk,
        by_xor(full_v).reshape(ways, -1),
        full_proj[None],
        by_xor(full_up).reshape(2 * ways, -1),
        full_down[None],
    )

    context = cond.reshape(micros * slots, width)
    act = jax.nn.silu(context.astype(F32)).astype(BF16)
    act_blocks = jnp.transpose(act.reshape(micros * slots, dps, width // dps), (1, 0, 2))
    act_all = send_dp(act_blocks)
    mod_terms = return_dp(dot(act_all, mod_w, "kgd,dm->kgm"))
    bias_mod = lax.dynamic_slice_in_dim(full_ada, own_t * mod_cols, mod_cols)
    mod_block = jnp.sum(mod_terms, axis=0) + bias_mod
    mod_rel = jnp.stack(send_tensor(mod_block.reshape(ways, share, mod_cols)))
    modulate = jnp.transpose(ordered(mod_rel), (1, 0, 2)).reshape(share, ways * mod_cols)

    mod6 = modulate.reshape(share, 6, width)

    half = hidden_cols // 2
    pack_shard = jnp.concatenate(
        [w_qkv[0, :, 0], w_qkv[0, :, 1], w_qkv[0, :, 2], w_proj[0].T], axis=1
    )
    pack_own = gather_dp(pack_shard)
    up_own = gather_dp(after(w_up[0], pack_own, tokens_in))
    qk_w = spread_tensor(pack_own[:, : 2 * qkv_cols], 1, 2)
    vp_w = spread_tensor(pack_own[:, 2 * qkv_cols :], 2, 1)
    down_own = gather_dp(after(w_down[0].T, up_own, mod6, qk_w[1], vp_w[2], bias_qk))
    up_a = spread_tensor(after(up_own[:, :half], qk_w[3], qk_w[2]), 1, 2)
    up_b = spread_tensor(after(up_own[:, half:], vp_w[3], vp_w[1]), 2, 1)
    down_a = spread_tensor(after(down_own[:, :half], up_a[1]), 1, 2)
    down_b = spread_tensor(after(down_own[:, half:], up_b[2]), 2, 1)
    interleave = lambda first, second: [piece for pair in zip(first, second) for piece in pair]
    up_w, down_w = interleave(up_a, up_b), interleave(down_a, down_b)
    weights = (qk_w, vp_w, up_w, down_w)

    slot_mask = (lax.broadcasted_iota(jnp.int32, (micros, slots), 1) < live).astype(F32)
    own_mask = pick(slot_mask.reshape(ways, share), own_t)

    def on_first(run, args, otherwise=None):
        shapes = jax.eval_shape(run, args)
        rest = (lambda args: zeros_like_shapes(shapes)) if otherwise is None else otherwise
        return lax.cond(is_first, run, rest, args)

    ahead = on_first(
        lambda args: attend_forward(*args), (tokens_in, mod6, (qk_w, vp_w), biases)
    )
    normed_a, qk, value, attended, branch, middle, normed_b = ahead
    lifted, hidden, second, output_first = on_first(
        lambda args: lift_forward(*args), (normed_b, middle, mod6, weights, biases)
    )
    saved_a = (normed_a, qk, value, attended, branch)
    saved_b = (middle, normed_b, lifted, hidden, second)
    arrived = lax.ppermute(output_first, "section", [(0, 1)])

    def second_layer(args):
        arrived, tokens, mask, mod6, weights, biases = args
        output, saved_a, saved_b = layer_forward(arrived, mod6, weights, biases)
        grad_out = tokens * mask[:, None, None].astype(BF16)
        grad_middle, kept_b, sums_b = lift_backward(grad_out, mod6, weights, saved_b)
        grad_input, kept_a, sums_a = attend_backward(grad_middle, arrived, mod6, weights, saved_a)
        return output, grad_input, kept_a, kept_b, sums_a, sums_b

    args = (arrived, tokens_in, own_mask, mod6, weights, biases)
    shapes = jax.eval_shape(second_layer, args)
    output_second, grad_second_in, kept_a1, kept_b1, sums_a1, sums_b1 = lax.cond(
        is_first, lambda args: zeros_like_shapes(shapes), second_layer, args
    )
    back = lax.ppermute(grad_second_in, "section", [(1, 0)])

    pieces = len(up_w)

    def first_lift(args):
        back, mod6, weights, saved_b = args[:4]
        grad_middle, kept_b, sums_b = lift_backward(back, mod6, weights, saved_b)
        return grad_middle, sums_b, lift_weights(kept_b, pieces)

    def second_lift(args):
        kept_b1, sums_b1, saved_b = args[4], args[5], args[3]
        return jnp.zeros_like(saved_b[0]), sums_b1, lift_weights(kept_b1, pieces)

    args = (back, mod6, weights, saved_b, kept_b1, sums_b1)
    grad_middle, sums_b, lift_slabs = on_first(first_lift, args, second_lift)

    def first_attend(args):
        grad_middle, tokens, mod6, weights, saved_a = args[:5]
        grad_input, kept_a, sums_a = attend_backward(grad_middle, tokens, mod6, weights, saved_a)
        return grad_input, sums_a, attend_weights(kept_a)

    def second_attend(args):
        kept_a1, sums_a1, grad_second_in = args[5:]
        return grad_second_in, sums_a1, attend_weights(kept_a1)

    args = (grad_middle, tokens_in, mod6, weights, saved_a, kept_a1, sums_a1, grad_second_in)
    grad_input, sums_a, attend_slabs = on_first(first_attend, args, second_attend)
    output = jnp.where(is_first, output_first, output_second)

    g_up, g_down = lift_slabs[:pieces], lift_slabs[pieces:]
    g_qk, g_vp = attend_slabs[:ways], attend_slabs[ways:]
    pair = lambda first, second: jnp.concatenate([first, second], axis=1)
    out_down = scatter_dp(
        pair(collect_tensor(g_down[::2], 1, 2), collect_tensor(g_down[1::2], 2, 1))
    )
    out_up = scatter_dp(pair(collect_tensor(g_up[::2], 1, 2), collect_tensor(g_up[1::2], 2, 1)))
    out_pack = scatter_dp(pair(collect_tensor(g_qk, 1, 2), collect_tensor(g_vp, 2, 1)))
    shard_qkv = out_pack[:, : 3 * qkv_cols].reshape(-1, 3, qkv_cols)
    shard_proj = out_pack[:, 3 * qkv_cols :].T
    shard_up = out_up
    shard_down = out_down.T

    grad_mod = jnp.concatenate([sums_a[0][:, :3], sums_b[0][:, :3]], axis=1)
    grad_mod = grad_mod.reshape(share, 6 * width).astype(BF16)

    grad_groups = jnp.transpose(grad_mod.reshape(share, ways, mod_cols), (1, 0, 2))
    grad_block = ordered(jnp.stack(send_tensor(grad_groups)))
    grad_all = share_dp(grad_block.reshape(micros * slots, mod_cols))
    shard_ada = dot(act_all, grad_all, "kgd,kgm->dm")
    ctx_terms = return_dp(dot(grad_all, mod_w, "kgm,dm->kgd").astype(BF16))
    ctx = jnp.transpose(ctx_terms, (1, 0, 2)).reshape(micros * slots, width)
    for axis, step in (("tensor", 1), ("tensor", 2), ("section", 1)):
        if axis == "section":
            ctx = after(ctx, out_pack, out_up, out_down)
        ctx = (ctx.astype(F32) + swap(ctx, axis, step).astype(F32)).astype(BF16)
    silu_back = jax.vjp(jax.nn.silu, cond.astype(F32))[1]
    cond_grad = silu_back(ctx.astype(F32).reshape(cond.shape))[0].astype(BF16)

    pack_sums = jnp.sum(sums_a[1], axis=0)
    parts = [
        by_xor(pack_sums[:ways, :qkv_cols].reshape(-1)),
        by_xor(pack_sums[ways:, :qkv_cols].reshape(-1)),
        jnp.sum(sums_a[0][:, 3], axis=0),
        by_xor(jnp.sum(sums_b[1], axis=0).reshape(-1)),
        jnp.sum(sums_b[0][:, 3], axis=0),
        jnp.sum(grad_mod.astype(F32), axis=0),
    ]
    bias_terms = jnp.concatenate([part.reshape(dps, ways, -1) for part in parts], axis=2)
    bias_terms = scatter_dp(bias_terms)[0]
    bias_out = sum(send_tensor(bias_terms))
    bias_pieces, start = [], 0
    for cut in cuts:
        bias_pieces.append(bias_out[start : start + cut])
        start += cut

    def handed_back(whole):
        split = jnp.transpose(whole.reshape(share, ways, tokens_own, width), (1, 0, 2, 3))
        arrivals = [split[0]] + [swap(split[j], "tensor", j) for j in range(1, ways)]
        return ordered(jnp.stack(arrivals)).reshape(latents.shape)

    layer_out = handed_back(output)
    input_grad = handed_back(grad_input)
    return (
        layer_out[None],
        input_grad[None],
        cond_grad,
        shard_qkv[None],
        shard_proj[None],
        shard_up[None],
        shard_down[None],
        shard_ada[None],
        jnp.stack(bias_pieces[:2])[None],
        bias_pieces[2][None],
        bias_pieces[3][None],
        bias_pieces[4][None],
        bias_pieces[5][None],
    )


def solution(mesh):
    both = ("dp", "tensor")
    return jax.shard_map(
        body,
        mesh=mesh,
        in_specs=(
            P(None, "dp", "tensor", None),
            P(None, "dp", None),
            P(None, "dp", "tensor", None),
            P(None, "dp"),
            P("section", "dp", None, "tensor"),
            P("section", "tensor", "dp"),
            P("section", "dp", "tensor"),
            P("section", "tensor", "dp"),
            P("section", "dp", "tensor"),
            P("section", None, both),
            P("section", both),
            P("section", both),
            P("section", both),
            P("section", both),
        ),
        out_specs=(
            P("section", None, "dp", "tensor", None),
            P("section", None, "dp", "tensor", None),
            P(None, "dp", None),
            P("section", "dp", None, "tensor"),
            P("section", "tensor", "dp"),
            P("section", "dp", "tensor"),
            P("section", "tensor", "dp"),
            P("section", "dp", "tensor"),
            P("section", None, both),
            P("section", both),
            P("section", both),
            P("section", both),
            P("section", both),
        ),
        check_vma=False,
    )
```

```python
import functools
import math

import jax
import jax.numpy as jnp
from jax import lax
from jax.experimental import pallas as pl
from jax.experimental.pallas import tpu as pltpu
from jax.sharding import PartitionSpec as P

HEAD_DIM = 64
BF16 = jnp.bfloat16
F32 = jnp.float32


def swap(shard, axis, step):
    peers = lax.axis_size(axis)
    return lax.ppermute(shard, axis, [(i, i ^ step) for i in range(peers)])


def turned(shard, axis, by):
    peers = lax.axis_size(axis)
    return lax.ppermute(shard, axis, [(i, (i + by) % peers) for i in range(peers)])


def pick(blocks, index):
    return lax.dynamic_index_in_dim(blocks, index, 0, keepdims=False)


def direct_dp():
    return lax.axis_size("dp") == 4


def gather_dp(shard):
    peers = lax.axis_size("dp")
    if not direct_dp():
        return lax.all_gather(shard, "dp")
    place = lax.axis_index("dp")
    whole = jnp.zeros((peers,) + shard.shape, shard.dtype)
    for k in range(peers):
        piece = shard if k == 0 else turned(shard, "dp", k)
        whole = lax.dynamic_update_index_in_dim(whole, piece, (place - k) % peers, 0)
    return whole


def ordered(blocks):
    own = lax.axis_index("tensor")
    return jnp.stack([pick(blocks, b ^ own) for b in range(blocks.shape[0])])


def send_tensor(blocks):
    own = lax.axis_index("tensor")
    return [pick(blocks, own)] + [
        swap(pick(blocks, own ^ j), "tensor", j) for j in range(1, lax.axis_size("tensor"))
    ]


def spread_tensor(own, first, second):
    near = swap(own, "tensor", first)
    side = swap(own, "tensor", second)
    far = swap(near, "tensor", second)
    pieces = {0: own, first: near, second: side, first ^ second: far}
    return [pieces[j] for j in range(4)]


def first_hop(sent, kept, step):
    near = swap(sent, "tensor", step)
    rest = kept.shape[0] // 2
    return near, (kept[rest:].astype(F32) + near[rest:].astype(F32)).astype(BF16)


def second_hop(kept, near, onward, step):
    far = swap(onward, "tensor", step)
    rest = kept.shape[0] // 2
    return (kept[:rest].astype(F32) + near[:rest].astype(F32) + far.astype(F32)).astype(BF16)


def scatter_rows(parts):
    peers = lax.axis_size("dp")
    if not direct_dp():
        whole = jnp.concatenate(parts)
        return lax.psum_scatter(whole, "dp", scatter_dimension=1, tiled=True).astype(F32)
    place = lax.axis_index("dp")
    rows = parts[0].shape[1] // peers
    block = lambda at: jnp.concatenate(
        [lax.dynamic_slice_in_dim(part, at * rows, rows, 1) for part in parts]
    )
    total = block(place).astype(F32)
    for k in range(1, peers):
        total = total + turned(block((place + k) % peers), "dp", k).astype(F32)
    return total


VMEM_BYTES = 50 * 1024 * 1024
GELU_A = 0.7978845608028654
GELU_B = 0.044715


def dot(lhs, rhs, spec):
    return jnp.einsum(spec, lhs, rhs, preferred_element_type=F32)


def mm(lhs, rhs):
    return jnp.dot(lhs, rhs, preferred_element_type=F32)


def mm_nt(lhs, rhs):
    return lax.dot_general(lhs, rhs, (((1,), (1,)), ((), ())), preferred_element_type=F32)


def mm_tn(lhs, rhs):
    return lax.dot_general(lhs, rhs, (((0,), (0,)), ((), ())), preferred_element_type=F32)


def norm_parts(features):
    centred = features - jnp.mean(features, axis=-1, keepdims=True)
    spread = jnp.mean(centred * centred, axis=-1, keepdims=True)
    rate = lax.rsqrt(spread + 1e-06)
    return centred * rate, rate


def norm_back(unit, rate, grad):
    lean = jnp.mean(grad, axis=-1, keepdims=True)
    tilt = jnp.mean(grad * unit, axis=-1, keepdims=True)
    return rate * (grad - lean - unit * tilt)


def token_sum(part):
    return jnp.sum(part, axis=0, keepdims=True)


def head_cols(block, start, head):
    return block[:, start + head * HEAD_DIM : start + (head + 1) * HEAD_DIM]


def attend_kernel(ways, heads, refs):
    x_ref, mod_ref, bqk_ref, bv_ref, bproj_ref = refs[:5]
    pack_w = refs[5 : 5 + ways]
    na_ref, qk_ref, v_ref, att_ref, branch_ref, middle_ref, nb_ref = refs[5 + ways :]
    cols = heads * HEAD_DIM
    width = x_ref.shape[2]
    scale = HEAD_DIM**-0.5
    x = x_ref[0].astype(F32)
    shift_a, scale_a, gate_a = (mod_ref[0, i : i + 1, :] for i in range(3))
    shift_b, scale_b = (mod_ref[0, i : i + 1, :] for i in (3, 4))
    normed = (norm_parts(x)[0] * (1.0 + scale_a) + shift_a).astype(BF16)
    na_ref[0] = normed
    branch = jnp.zeros_like(x) + bproj_ref[...]
    for j in range(ways):
        qk = (mm(normed, pack_w[j][:width, : 2 * cols]) + bqk_ref[j : j + 1, :]).astype(BF16)
        value = (mm(normed, pack_w[j][:width, 2 * cols : 3 * cols]) + bv_ref[j : j + 1, :]).astype(BF16)
        qk_ref[0, j] = qk
        v_ref[0, j] = value
        outs = [jnp.zeros((x.shape[0], cols), F32)]
        for h in range(heads):
            query = head_cols(qk, 0, h) * jnp.asarray(scale, BF16)
            scores = mm_nt(query, head_cols(qk, cols, h))
            raised = jnp.exp(scores - jnp.max(scores, axis=-1, keepdims=True))
            total = jnp.sum(raised, axis=-1, keepdims=True)
            outs.append(mm(raised.astype(BF16), head_cols(value, 0, h)) * (1.0 / total))
        padded = jnp.concatenate(outs, axis=1).astype(BF16)
        att_ref[0, j] = padded
        branch = branch + mm_nt(padded, pack_w[j][:width, 2 * cols :])
    branch_ref[0] = branch.astype(BF16)
    middle = x + gate_a * branch
    middle_ref[0] = middle
    nb_ref[0] = (norm_parts(middle)[0] * (1.0 + scale_b) + shift_b).astype(BF16)


def lift_kernel(pieces, refs):
    nb_ref, middle_ref, mod_ref, bup_ref, bdown_ref = refs[:5]
    both_w = refs[5 : 5 + pieces]
    lifted_ref, hidden_ref, second_ref, out_ref = refs[5 + pieces :]
    normed = nb_ref[0]
    middle = middle_ref[0]
    gate_b = mod_ref[0, 5:6, :]
    second = jnp.zeros_like(middle) + bdown_ref[...]
    for c in range(pieces):
        part = both_w[c].shape[2]
        lifted = mm(normed, both_w[c][0]) + bup_ref[c : c + 1, :]
        turn = jnp.tanh(GELU_A * (lifted + GELU_B * lifted * lifted * lifted))
        hidden = (0.5 * lifted * (1.0 + turn)).astype(BF16)
        lifted_ref[0, :, c * part : (c + 1) * part] = lifted.astype(BF16)
        hidden_ref[0, :, c * part : (c + 1) * part] = hidden
        second = second + mm_nt(hidden, both_w[c][1])
    second_ref[0] = second.astype(BF16)
    out_ref[0] = (middle + gate_b * second).astype(BF16)


def lift_back_kernel(pieces, refs):
    g_ref, second_ref, lifted_ref, middle_ref, mod_ref = refs[:5]
    both_w = refs[5 : 5 + pieces]
    gs_ref, gl_ref, gm_ref, sums_ref, lift_sums_ref = refs[5 + pieces :]
    grad = g_ref[0].astype(F32)
    scale_b, gate_b = mod_ref[0, 4:5, :], mod_ref[0, 5:6, :]
    grad_second = (gate_b * grad).astype(BF16)
    gs_ref[0] = grad_second
    normed = jnp.zeros_like(grad)
    for c in range(pieces):
        part = both_w[c].shape[2]
        grad_hidden = mm(grad_second, both_w[c][1])
        v = lifted_ref[0, :, c * part : (c + 1) * part].astype(F32)
        square = v * v
        turn = jnp.tanh(GELU_A * v * (1.0 + GELU_B * square))
        slope = 0.5 * (1.0 + turn) + (0.5 * GELU_A) * v * (1.0 - turn * turn) * (
            1.0 + (3.0 * GELU_B) * square
        )
        grad_lifted = (grad_hidden * slope).astype(BF16)
        gl_ref[0, :, c * part : (c + 1) * part] = grad_lifted
        lift_sums_ref[0, c : c + 1, :] = token_sum(grad_lifted.astype(F32))
        normed = normed + mm_nt(grad_lifted, both_w[c][0])
    unit, rate = norm_parts(middle_ref[0])
    gm_ref[0] = grad + norm_back(unit, rate, normed * (1.0 + scale_b))
    sums_ref[0, 0:1, :] = token_sum(normed)
    sums_ref[0, 1:2, :] = token_sum(normed * unit)
    sums_ref[0, 2:3, :] = token_sum(grad * second_ref[0].astype(F32))
    sums_ref[0, 3:4, :] = token_sum(grad_second.astype(F32))


def attend_back_kernel(ways, heads, refs):
    gm_ref, branch_ref, qk_ref, v_ref, x_ref, mod_ref = refs[:6]
    pack_w = refs[6 : 6 + ways]
    gb_ref, gqk_ref, gv_ref, gi_ref, sums_ref, pack_sums_ref = refs[6 + ways :]
    cols = heads * HEAD_DIM
    width = gm_ref.shape[2]
    scale = HEAD_DIM**-0.5
    middle = gm_ref[0]
    scale_a, gate_a = mod_ref[0, 1:2, :], mod_ref[0, 2:3, :]
    grad_branch = (gate_a * middle).astype(BF16)
    gb_ref[0] = grad_branch
    normed = jnp.zeros_like(middle)
    for j in range(ways):
        grad_att = mm(grad_branch, pack_w[j][:width, 2 * cols :]).astype(BF16)
        qk = qk_ref[0, j]
        value = v_ref[0, j]
        grads_q, grads_k, grads_v = [], [], []
        for h in range(heads):
            query, key = head_cols(qk, 0, h), head_cols(qk, cols, h)
            grad_head = head_cols(grad_att, cols, h)
            scores = mm_nt(key, query * jnp.asarray(scale, BF16))
            raised = jnp.exp(scores - jnp.max(scores, axis=0, keepdims=True))
            probs = raised * (1.0 / jnp.sum(raised, axis=0, keepdims=True))
            grads_v.append(mm(probs.astype(BF16), grad_head))
            grad_probs = mm_nt(head_cols(value, 0, h), grad_head)
            total = jnp.sum(grad_probs * probs, axis=0, keepdims=True)
            grad_scores = (probs * (grad_probs - total)).astype(BF16)
            grads_k.append(mm(grad_scores, query) * scale)
            grads_q.append(mm_tn(grad_scores, key) * scale)
        grad_qk = jnp.concatenate(grads_q + grads_k, axis=1).astype(BF16)
        grads_v.append(jnp.zeros((middle.shape[0], cols), F32))
        grad_v = jnp.concatenate(grads_v, axis=1).astype(BF16)
        gqk_ref[0, j] = grad_qk
        gv_ref[0, j] = grad_v
        pack_sums_ref[0, j : j + 1, :] = token_sum(grad_qk.astype(F32))
        pack_sums_ref[0, ways + j : ways + j + 1, :] = token_sum(grad_v.astype(F32))
        normed = normed + mm_nt(grad_qk, pack_w[j][:width, : 2 * cols])
        normed = normed + mm_nt(grad_v, pack_w[j][:width, 2 * cols :])
    unit, rate = norm_parts(x_ref[0].astype(F32))
    gi_ref[0] = (middle + norm_back(unit, rate, normed * (1.0 + scale_a))).astype(BF16)
    sums_ref[0, 0:1, :] = token_sum(normed)
    sums_ref[0, 1:2, :] = token_sum(normed * unit)
    sums_ref[0, 2:3, :] = token_sum(middle * branch_ref[0].astype(F32))
    sums_ref[0, 3:4, :] = token_sum(grad_branch.astype(F32))


def flat_tokens(ref):
    return ref[...].reshape(ref.shape[0] * ref.shape[1], ref.shape[2])


SENT = {1: (1, 3), 2: (2, 3)}
KEPT = {1: (0, 2), 2: (0, 1)}


def lift_weights_kernel(refs):
    nb_ref, gl_ref, gs_ref, hidden_ref = refs[:4]
    outs = {1: refs[4:6], 2: refs[6:8]}
    part = refs[4].shape[2]
    for kind, (left_ref, right_ref) in enumerate(((gs_ref, hidden_ref), (nb_ref, gl_ref))):
        left = flat_tokens(left_ref).T
        for side, first in enumerate((1, 2)):
            for place, blocks in enumerate((SENT[first], KEPT[first])):
                for i, j in enumerate(blocks):
                    c = 2 * j + side
                    right = right_ref[:, :, c * part : (c + 1) * part]
                    right = right.reshape(right.shape[0] * right.shape[1], part)
                    outs[first][place][2 * i + kind] = mm(left, right).astype(BF16)


def attend_weights_kernel(refs):
    na_ref, gqk_ref, gv_ref, gb_ref, att_ref = refs[:5]
    outs = {1: refs[5:7], 2: refs[7:9]}
    latents = na_ref.shape[0]
    left_n = flat_tokens(na_ref).T
    left_b = flat_tokens(gb_ref).T
    over = lambda ref, j: jnp.concatenate([ref[g, j] for g in range(latents)], axis=0)
    for place in range(2):
        for i, j in enumerate((SENT, KEPT)[place][1]):
            outs[1][place][i] = mm(left_n, over(gqk_ref, j)).astype(BF16)
        for i, j in enumerate((SENT, KEPT)[place][2]):
            grad = mm(left_n, over(gv_ref, j)) + mm(left_b, over(att_ref, j))
            outs[2][place][i] = grad.astype(BF16)


def per_latent(shape):
    rank = len(shape)
    return pl.BlockSpec((1,) + tuple(shape[1:]), lambda g: (g,) + (0,) * (rank - 1))


def constant(shape):
    rank = len(shape)
    return pl.BlockSpec(tuple(shape), lambda g: (0,) * rank, pipeline_mode=pl.Buffered(1))


def over_latents(kernel, name, varying, fixed, outs, flops, run=None, others=()):
    flags = [] if run is None else [run]

    def whole(*refs):
        refs = refs[len(flags) :]
        ins, rest = refs[: len(varying)], refs[len(varying) : len(varying) + len(fixed)]
        kernel(ins + rest + refs[-len(outs) :])

    def flagged(*refs):
        flag = refs[0][0]

        @pl.when(flag == 1)
        def _():
            whole(*refs)

        if others:

            @pl.when(flag == 0)
            def _():
                start = 1 + len(varying) + len(fixed)
                for source, target in zip(refs[start : start + len(others)], refs[-len(outs) :]):
                    target[...] = source[...]

    return pl.pallas_call(
        flagged if flags else whole,
        grid=(varying[0].shape[0],),
        in_specs=[pl.BlockSpec(memory_space=pltpu.SMEM)] * len(flags)
        + [per_latent(a.shape) for a in varying]
        + [constant(a.shape) for a in fixed]
        + [per_latent(a.shape) for a in others],
        out_specs=[per_latent(shape) for shape, _ in outs],
        out_shape=[jax.ShapeDtypeStruct(shape, dtype) for shape, dtype in outs],
        compiler_params=pltpu.CompilerParams(vmem_limit_bytes=VMEM_BYTES),
        cost_estimate=pl.CostEstimate(
            flops=flops,
            bytes_accessed=sum(a.size * a.dtype.itemsize for a in varying + fixed)
            + sum(2 * math.prod(shape) for shape, _ in outs),
            transcendentals=0,
        ),
        name=name,
    )(*flags, *varying, *fixed, *others)


def at_once(kernel, name, inputs, out_shapes, flops):
    return pl.pallas_call(
        lambda *refs: kernel(refs),
        in_specs=[pl.BlockSpec(memory_space=pltpu.VMEM)] * len(inputs),
        out_specs=[pl.BlockSpec(memory_space=pltpu.VMEM)] * len(out_shapes),
        out_shape=[jax.ShapeDtypeStruct(shape, BF16) for shape in out_shapes],
        compiler_params=pltpu.CompilerParams(vmem_limit_bytes=VMEM_BYTES),
        cost_estimate=pl.CostEstimate(
            flops=flops,
            bytes_accessed=sum(a.size * a.dtype.itemsize for a in inputs)
            + sum(2 * math.prod(shape) for shape in out_shapes),
            transcendentals=0,
        ),
        name=name,
    )(*inputs)


def attend_forward(tokens_in, mod6, weights, biases):
    pack_w = weights[0]
    b_qk, b_v, b_proj = biases[:3]
    ways, cols = len(pack_w), b_v.shape[1]
    latents, tokens, width = tokens_in.shape
    whole = (latents, tokens, width)
    return over_latents(
        functools.partial(attend_kernel, ways, cols // HEAD_DIM),
        "attend_forward",
        [tokens_in, mod6],
        [b_qk, b_v, b_proj, *pack_w],
        [
            (whole, BF16),
            ((latents, ways, tokens, 2 * cols), BF16),
            ((latents, ways, tokens, cols), BF16),
            ((latents, ways, tokens, 2 * cols), BF16),
            (whole, BF16),
            (whole, F32),
            (whole, BF16),
        ],
        10 * latents * tokens * width * width,
    )


def lift_forward(normed_b, middle, mod6, weights, biases):
    both_w = weights[1]
    b_up, b_down = biases[3:]
    whole = middle.shape
    wide = whole[:2] + (b_up.size,)
    return over_latents(
        functools.partial(lift_kernel, len(both_w)),
        "lift_forward",
        [normed_b, middle, mod6],
        [b_up, b_down, *both_w],
        [(wide, BF16), (wide, BF16), (whole, BF16), (whole, BF16)],
        4 * math.prod(whole) * b_up.size,
    )


def layer_forward(tokens_in, mod6, weights, biases):
    normed_a, qk, value, attended, branch, middle, normed_b = attend_forward(
        tokens_in, mod6, weights, biases
    )
    lifted, hidden, second, output = lift_forward(normed_b, middle, mod6, weights, biases)
    saved_a = (normed_a, qk, value, attended, branch)
    saved_b = (middle, normed_b, lifted, hidden, second)
    return output, saved_a, saved_b


def lift_backward(grad_out, mod6, weights, saved_b, run, others=()):
    both_w = weights[1]
    middle, normed_b, lifted, hidden, second = saved_b
    latents, tokens, width = middle.shape
    grad_second, grad_lifted, grad_middle, sums, lift_sums = over_latents(
        functools.partial(lift_back_kernel, len(both_w)),
        "lift_backward",
        [grad_out, second, lifted, middle, mod6],
        both_w,
        [
            (middle.shape, BF16),
            (lifted.shape, BF16),
            (middle.shape, F32),
            ((latents, 4, width), F32),
            ((latents, len(both_w), both_w[0].shape[2]), F32),
        ],
        4 * middle.size * lifted.shape[2],
        run,
        others,
    )
    outs = (grad_second, grad_lifted, grad_middle, sums, lift_sums)
    return outs, (normed_b, grad_lifted, grad_second, hidden)


def attend_backward(grad_middle, tokens_in, mod6, weights, saved_a, run, others=()):
    pack_w = weights[0]
    normed_a, qk, value, attended, branch = saved_a
    latents, tokens, width = grad_middle.shape
    cols = value.shape[3]
    grad_branch, grad_qk, grad_v, grad_input, sums, pack_sums = over_latents(
        functools.partial(attend_back_kernel, len(pack_w), cols // HEAD_DIM),
        "attend_backward",
        [grad_middle, branch, qk, value, tokens_in, mod6],
        pack_w,
        [
            (grad_middle.shape, BF16),
            (qk.shape, BF16),
            (qk.shape, BF16),
            (grad_middle.shape, BF16),
            ((latents, 4, width), F32),
            ((latents, 2 * len(pack_w), 2 * cols), F32),
        ],
        16 * grad_middle.size * width,
        run,
        others,
    )
    outs = (grad_branch, grad_qk, grad_v, grad_input, sums, pack_sums)
    return outs, (normed_a, grad_qk, grad_v, grad_branch, attended)


def lift_weights(kept):
    normed_b, grad_lifted = kept[:2]
    width, wide = normed_b.shape[2], grad_lifted.shape[2]
    shape = (4, width, wide // 8)
    return at_once(lift_weights_kernel, "lift_weights", kept, [shape] * 4, 4 * normed_b.size * wide)


def attend_weights(kept):
    normed_a, grad_qk = kept[:2]
    shape = (2, normed_a.shape[2], grad_qk.shape[3])
    flops = 6 * normed_a.size * grad_qk.shape[1] * grad_qk.shape[3]
    return at_once(attend_weights_kernel, "attend_weights", kept, [shape] * 4, flops)


def after(value, *others):
    return lax.optimization_barrier((value, others))[0]


def body(
    latents,
    cond,
    cotangent,
    live,
    w_qkv,
    w_proj,
    w_up,
    w_down,
    w_ada,
    bias_qv,
    bias_proj,
    bias_up,
    bias_down,
    bias_ada,
):
    micros, slots, tokens_own, width = latents.shape
    ways = lax.axis_size("tensor")
    dps = lax.axis_size("dp")
    share = micros * slots // ways
    own_t = lax.axis_index("tensor")
    is_first = lax.axis_index("section") == 0
    qkv_cols = w_qkv.shape[3]
    hidden_cols = w_up.shape[2]
    mod_cols = w_ada.shape[2]
    mod_w = w_ada[0]

    source = jnp.where(is_first, latents, cotangent).reshape(ways, share, tokens_own, width)
    tokens_in = jnp.concatenate(send_tensor(source), axis=1)

    half = hidden_cols // 2
    pair_cols = 2 * qkv_cols
    rows = width // dps
    pack_shard = jnp.concatenate(
        [w_qkv[0, :, 0], w_qkv[0, :, 1], w_qkv[0, :, 2], w_proj[0].T], axis=1
    )
    bias_shard = jnp.concatenate(
        [bias_qv[0, 0], bias_qv[0, 1], bias_proj[0], bias_up[0], bias_down[0], bias_ada[0]]
    )
    cuts = [bias_qv.shape[2]] * 2 + [b.shape[1] for b in (bias_proj, bias_up, bias_down, bias_ada)]
    bias_size = sum(cuts)
    latent_count = micros * slots
    act = jax.nn.silu(cond.astype(F32)).astype(BF16).reshape(latent_count, width)
    riders = jnp.concatenate([jnp.pad(bias_shard, (0, width - bias_size))[None], act])
    riders = jnp.pad(riders, ((0, -riders.shape[0] % 16), (0, 0)))
    first_kind = gather_dp(jnp.concatenate([pack_shard, riders]))
    bias_dp = first_kind[:, rows, :bias_size].reshape(-1)
    bias_dp = jnp.pad(bias_dp, (0, -bias_dp.shape[0] % (16 * 2 * pair_cols)))
    pack_own = jnp.concatenate(
        [first_kind[:, :rows].reshape(width, 2 * pair_cols), bias_dp.reshape(-1, 2 * pair_cols)]
    )
    act_all = lax.dynamic_slice_in_dim(
        first_kind[:, rows + 1 : rows + 1 + latent_count],
        lax.axis_index("dp") * rows,
        rows,
        2,
    )
    pack_own = after(pack_own, tokens_in)
    pack_w = [pack_own] + [swap(pack_own, "tensor", j) for j in range(1, ways)]
    second_kind = gather_dp(after(jnp.stack([w_up[0], w_down[0].T]), pack_own))
    mod_terms = dot(after(act_all, second_kind), mod_w, "kgd,dm->kgm")
    mod_block = jnp.sum(lax.all_to_all(mod_terms, "dp", 0, 0), axis=0)
    mod_block = lax.all_to_all(mod_block.reshape(ways, share, mod_cols), "tensor", 0, 0)
    both_own = jnp.transpose(second_kind, (1, 0, 2, 3)).reshape(2, width, hidden_cols)

    bias_rel = jnp.stack([part[width:].reshape(-1)[: dps * bias_size] for part in pack_w])
    bias_all = ordered(bias_rel).reshape(ways, dps, bias_size)
    bias_all = jnp.transpose(bias_all, (1, 0, 2)).astype(F32)
    full, start = [], 0
    for cut in cuts:
        full.append(bias_all[:, :, start : start + cut].reshape(-1))
        start += cut
    full_q, full_v, full_proj, full_up, full_down, full_ada = full
    by_xor = lambda vector: ordered(vector.reshape(ways, -1)).reshape(-1)
    bias_qk = by_xor(full_q).reshape(ways, -1)
    bias_qk = jnp.concatenate([bias_qk, jnp.zeros_like(bias_qk)], axis=1)
    biases = (
        bias_qk,
        by_xor(full_v).reshape(ways, -1),
        full_proj[None],
        by_xor(full_up).reshape(2 * ways, -1),
        full_down[None],
    )

    modulate = jnp.transpose(mod_block, (1, 0, 2)).reshape(share, ways * mod_cols) + full_ada
    mod6 = modulate.reshape(share, 6, width)

    both_a = spread_tensor(after(both_own[:, :, :half], pack_w), 1, 2)
    both_b = spread_tensor(after(both_own[:, :, half:], pack_w), 2, 1)
    weights = (pack_w, [piece for pair in zip(both_a, both_b) for piece in pair])

    slot_mask = (lax.broadcasted_iota(jnp.int32, (micros, slots), 1) < live).astype(F32)
    own_mask = pick(slot_mask.reshape(ways, share), own_t)

    on_first = jnp.where(is_first, 1, 0).astype(jnp.int32).reshape(1)

    def handed_back(whole):
        split = jnp.transpose(whole.reshape(share, ways, tokens_own, width), (1, 0, 2, 3))
        arrivals = [split[0]] + [swap(split[j], "tensor", j) for j in range(1, ways)]
        return ordered(jnp.stack(arrivals)).reshape(latents.shape)

    output_first = layer_forward(tokens_in, mod6, weights, biases)[0]
    arrived = lax.ppermute(output_first, "section", [(0, 1)])
    incoming = jnp.where(is_first, tokens_in, arrived)
    output, saved_a, saved_b = layer_forward(incoming, mod6, weights, biases)

    grad_out = tokens_in * own_mask[:, None, None].astype(BF16)
    lift_1, _ = lift_backward(grad_out, mod6, weights, saved_b, 1 - on_first)
    attend_1, _ = attend_backward(lift_1[2], incoming, mod6, weights, saved_a, 1 - on_first)
    back = lax.ppermute(attend_1[3], "section", [(1, 0)])

    layer_out = handed_back(output)
    back = after(back, layer_out)
    lift_outs, kept_b = lift_backward(back, mod6, weights, saved_b, on_first, lift_1)
    lift_slabs = lift_weights(kept_b)
    attend_outs, kept_a = attend_backward(
        after(lift_outs[2], lift_slabs), incoming, mod6, weights, saved_a, on_first, attend_1
    )
    sums_b = lift_outs[3:]
    grad_input, sums_a = attend_outs[3], attend_outs[4:]
    attend_slabs = attend_weights(kept_a)
    near_a, onward_a = first_hop(*lift_slabs[:2], 1)
    near_b, onward_b = first_hop(*lift_slabs[2:], 2)
    sums_a, sums_b = after((sums_a, sums_b), onward_a, onward_b)

    grad_mod = jnp.concatenate([sums_a[0][:, :3], sums_b[0][:, :3]], axis=1)
    grad_mod = grad_mod.reshape(share, 6 * width).astype(BF16)

    pack_sums = jnp.sum(sums_a[1], axis=0)
    parts = [
        by_xor(pack_sums[:ways, :qkv_cols].reshape(-1)),
        by_xor(pack_sums[ways:, :qkv_cols].reshape(-1)),
        jnp.sum(sums_a[0][:, 3], axis=0),
        by_xor(jnp.sum(sums_b[1], axis=0).reshape(-1)),
        jnp.sum(sums_b[0][:, 3], axis=0),
        jnp.sum(grad_mod.astype(F32), axis=0),
    ]
    bias_terms = jnp.concatenate([part.reshape(dps, ways, -1) for part in parts], axis=2)
    bias_terms = jnp.transpose(bias_terms, (1, 0, 2)).reshape(ways, -1)
    grad_groups = jnp.transpose(grad_mod.reshape(share, ways, mod_cols), (1, 0, 2))
    grad_groups = grad_groups.reshape(ways, -1).astype(F32)
    mod_size = grad_groups.shape[1]
    arrivals = jnp.concatenate([grad_groups, bias_terms], axis=1)
    arrivals = lax.all_to_all(arrivals, "tensor", 0, 0)
    grad_block = arrivals[:, :mod_size].reshape(latent_count, mod_cols)
    bias_terms = jnp.sum(arrivals[:, mod_size:], axis=0).reshape(dps, bias_size)

    grad_block = jnp.broadcast_to(grad_block.reshape(1, -1), (dps, grad_block.size))
    shared = lax.all_to_all(jnp.concatenate([grad_block, bias_terms], axis=1), "dp", 0, 0)
    grad_all = shared[:, : -bias_size].reshape(dps, latent_count, mod_cols).astype(BF16)
    bias_out = jnp.sum(shared[:, -bias_size:], axis=0)

    lift_a = second_hop(lift_slabs[1], near_a, after(onward_a, arrivals), 2)
    lift_b = second_hop(lift_slabs[3], near_b, after(onward_b, arrivals), 1)
    near_a, onward_a = first_hop(after(attend_slabs[0], arrivals), attend_slabs[1], 1)
    near_b, onward_b = first_hop(after(attend_slabs[2], arrivals), attend_slabs[3], 2)
    out_lift = scatter_rows([lift_a, lift_b])
    sum_qk = second_hop(attend_slabs[1], near_a, onward_a, 2)
    sum_vp = second_hop(attend_slabs[3], near_b, onward_b, 1)
    out_attend = scatter_rows(after([sum_qk, sum_vp], out_lift))
    shard_down = jnp.concatenate([out_lift[0], out_lift[2]], axis=1).T
    shard_up = jnp.concatenate([out_lift[1], out_lift[3]], axis=1)
    shard_qkv = jnp.concatenate([out_attend[0], out_attend[1][:, :qkv_cols]], axis=1)
    shard_qkv = shard_qkv.reshape(-1, 3, qkv_cols)
    shard_proj = out_attend[1][:, qkv_cols:].T

    shard_ada = dot(act_all, grad_all, "kgd,kgm->dm")
    ctx_terms = dot(after(grad_all, out_lift), mod_w, "kgm,dm->kgd").astype(BF16)
    ctx_terms = lax.all_to_all(ctx_terms, "dp", 0, 0)
    ctx = jnp.transpose(ctx_terms, (1, 0, 2)).reshape(latent_count, width)
    ctx, grad_input = after((ctx, grad_input), sum_qk, sum_vp)
    for axis, step in (("tensor", 1), ("tensor", 2), ("section", 1)):
        if axis == "section":
            ctx = after(ctx, out_attend, out_lift)
        ctx = (ctx.astype(F32) + swap(ctx, axis, step).astype(F32)).astype(BF16)
    silu_back = jax.vjp(jax.nn.silu, cond.astype(F32))[1]
    cond_grad = silu_back(ctx.astype(F32).reshape(cond.shape))[0].astype(BF16)
    bias_pieces, start = [], 0
    for cut in cuts:
        bias_pieces.append(bias_out[start : start + cut])
        start += cut

    input_grad = handed_back(grad_input)
    return (
        layer_out[None],
        input_grad[None],
        cond_grad,
        shard_qkv[None],
        shard_proj[None],
        shard_up[None],
        shard_down[None],
        shard_ada[None],
        jnp.stack(bias_pieces[:2])[None],
        bias_pieces[2][None],
        bias_pieces[3][None],
        bias_pieces[4][None],
        bias_pieces[5][None],
    )


def solution(mesh):
    both = ("dp", "tensor")
    return jax.shard_map(
        body,
        mesh=mesh,
        in_specs=(
            P(None, "dp", "tensor", None),
            P(None, "dp", None),
            P(None, "dp", "tensor", None),
            P(None, "dp"),
            P("section", "dp", None, "tensor"),
            P("section", "tensor", "dp"),
            P("section", "dp", "tensor"),
            P("section", "tensor", "dp"),
            P("section", "dp", "tensor"),
            P("section", None, both),
            P("section", both),
            P("section", both),
            P("section", both),
            P("section", both),
        ),
        out_specs=(
            P("section", None, "dp", "tensor", None),
            P("section", None, "dp", "tensor", None),
            P(None, "dp", None),
            P("section", "dp", None, "tensor"),
            P("section", "tensor", "dp"),
            P("section", "dp", "tensor"),
            P("section", "tensor", "dp"),
            P("section", "dp", "tensor"),
            P("section", None, both),
            P("section", both),
            P("section", both),
            P("section", both),
            P("section", both),
        ),
        check_vma=False,
    )
```

```python
import functools
import math

import jax
import jax.numpy as jnp
from jax import lax
from jax.experimental import pallas as pl
from jax.experimental.pallas import tpu as pltpu
from jax.sharding import PartitionSpec as P

HEAD_DIM = 64
BF16 = jnp.bfloat16
F32 = jnp.float32


def swap(shard, axis, step):
    peers = lax.axis_size(axis)
    return lax.ppermute(shard, axis, [(i, i ^ step) for i in range(peers)])


def turned(shard, axis, by):
    peers = lax.axis_size(axis)
    return lax.ppermute(shard, axis, [(i, (i + by) % peers) for i in range(peers)])


def pick(blocks, index):
    return lax.dynamic_index_in_dim(blocks, index, 0, keepdims=False)


def direct_dp():
    return lax.axis_size("dp") == 4


def gather_dp(shard):
    peers = lax.axis_size("dp")
    if not direct_dp():
        return lax.all_gather(shard, "dp")
    place = lax.axis_index("dp")
    whole = jnp.zeros((peers,) + shard.shape, shard.dtype)
    for k in range(peers):
        piece = shard if k == 0 else turned(shard, "dp", k)
        whole = lax.dynamic_update_index_in_dim(whole, piece, (place - k) % peers, 0)
    return whole


def ordered(blocks):
    own = lax.axis_index("tensor")
    return jnp.stack([pick(blocks, b ^ own) for b in range(blocks.shape[0])])


def send_tensor(blocks):
    own = lax.axis_index("tensor")
    return [pick(blocks, own)] + [
        swap(pick(blocks, own ^ j), "tensor", j) for j in range(1, lax.axis_size("tensor"))
    ]


def spread_tensor(own, first, second):
    near = swap(own, "tensor", first)
    side = swap(own, "tensor", second)
    far = swap(near, "tensor", second)
    pieces = {0: own, first: near, second: side, first ^ second: far}
    return [pieces[j] for j in range(4)]


def first_hop(sent, kept, step):
    near = swap(sent, "tensor", step)
    rest = kept.shape[0] // 2
    return near, (kept[rest:].astype(F32) + near[rest:].astype(F32)).astype(BF16)


def second_hop(kept, near, onward, step):
    far = swap(onward, "tensor", step)
    rest = kept.shape[0] // 2
    return (kept[:rest].astype(F32) + near[:rest].astype(F32) + far.astype(F32)).astype(BF16)


def scatter_rows(parts):
    peers = lax.axis_size("dp")
    if not direct_dp():
        whole = jnp.concatenate(parts)
        return lax.psum_scatter(whole, "dp", scatter_dimension=1, tiled=True).astype(F32)
    place = lax.axis_index("dp")
    rows = parts[0].shape[1] // peers
    block = lambda at: jnp.concatenate(
        [lax.dynamic_slice_in_dim(part, at * rows, rows, 1) for part in parts]
    )
    total = block(place).astype(F32)
    for k in range(1, peers):
        total = total + turned(block((place + k) % peers), "dp", k).astype(F32)
    return total


VMEM_BYTES = 34 * 1024 * 1024
GELU_A = 0.7978845608028654
GELU_B = 0.044715


def dot(lhs, rhs, spec):
    return jnp.einsum(spec, lhs, rhs, preferred_element_type=F32)


def mm(lhs, rhs):
    return jnp.dot(lhs, rhs, preferred_element_type=F32)


def mm_nt(lhs, rhs):
    return lax.dot_general(lhs, rhs, (((1,), (1,)), ((), ())), preferred_element_type=F32)


def mm_tn(lhs, rhs):
    return lax.dot_general(lhs, rhs, (((0,), (0,)), ((), ())), preferred_element_type=F32)


def norm_parts(features):
    centred = features - jnp.mean(features, axis=-1, keepdims=True)
    spread = jnp.mean(centred * centred, axis=-1, keepdims=True)
    rate = lax.rsqrt(spread + 1e-06)
    return centred * rate, rate


def norm_back(unit, rate, grad):
    lean = jnp.mean(grad, axis=-1, keepdims=True)
    tilt = jnp.mean(grad * unit, axis=-1, keepdims=True)
    return rate * (grad - lean - unit * tilt)


def token_sum(part):
    return jnp.sum(part, axis=0, keepdims=True)


def head_cols(block, start, head):
    return block[:, start + head * HEAD_DIM : start + (head + 1) * HEAD_DIM]


def attend_kernel(ways, heads, refs):
    x_ref, mod_ref, bqk_ref, bv_ref, bproj_ref = refs[:5]
    pack_w = refs[5 : 5 + ways]
    na_ref, qk_ref, v_ref, att_ref, branch_ref, middle_ref, nb_ref = refs[5 + ways :]
    cols = heads * HEAD_DIM
    width = x_ref.shape[2]
    scale = HEAD_DIM**-0.5
    x = x_ref[0].astype(F32)
    shift_a, scale_a, gate_a = (mod_ref[0, i : i + 1, :] for i in range(3))
    shift_b, scale_b = (mod_ref[0, i : i + 1, :] for i in (3, 4))
    normed = (norm_parts(x)[0] * (1.0 + scale_a) + shift_a).astype(BF16)
    na_ref[0] = normed
    branch = jnp.zeros_like(x) + bproj_ref[...]
    for j in range(ways):
        qk = (mm(normed, pack_w[j][:width, : 2 * cols]) + bqk_ref[j : j + 1, :]).astype(BF16)
        value = (mm(normed, pack_w[j][:width, 2 * cols : 3 * cols]) + bv_ref[j : j + 1, :]).astype(BF16)
        qk_ref[0, j] = qk
        v_ref[0, j] = value
        outs = [jnp.zeros((x.shape[0], cols), F32)]
        for h in range(heads):
            query = head_cols(qk, 0, h) * jnp.asarray(scale, BF16)
            scores = mm_nt(query, head_cols(qk, cols, h))
            raised = jnp.exp(scores - jnp.max(scores, axis=-1, keepdims=True))
            total = jnp.sum(raised, axis=-1, keepdims=True)
            outs.append(mm(raised.astype(BF16), head_cols(value, 0, h)) * (1.0 / total))
        padded = jnp.concatenate(outs, axis=1).astype(BF16)
        att_ref[0, j] = padded
        branch = branch + mm_nt(padded, pack_w[j][:width, 2 * cols :])
    branch_ref[0] = branch.astype(BF16)
    middle = x + gate_a * branch
    middle_ref[0] = middle
    nb_ref[0] = (norm_parts(middle)[0] * (1.0 + scale_b) + shift_b).astype(BF16)


def lift_kernel(pieces, refs):
    nb_ref, middle_ref, mod_ref, bup_ref, bdown_ref = refs[:5]
    both_w = refs[5 : 5 + pieces]
    lifted_ref, hidden_ref, second_ref, out_ref = refs[5 + pieces :]
    normed = nb_ref[0]
    middle = middle_ref[0]
    gate_b = mod_ref[0, 5:6, :]
    second = jnp.zeros_like(middle) + bdown_ref[...]
    for c in range(pieces):
        part = both_w[c].shape[2]
        lifted = mm(normed, both_w[c][0]) + bup_ref[c : c + 1, :]
        turn = jnp.tanh(GELU_A * (lifted + GELU_B * lifted * lifted * lifted))
        hidden = (0.5 * lifted * (1.0 + turn)).astype(BF16)
        lifted_ref[0, :, c * part : (c + 1) * part] = lifted.astype(BF16)
        hidden_ref[0, :, c * part : (c + 1) * part] = hidden
        second = second + mm_nt(hidden, both_w[c][1])
    second_ref[0] = second.astype(BF16)
    out_ref[0] = (middle + gate_b * second).astype(BF16)


def lift_back_kernel(pieces, refs):
    g_ref, second_ref, lifted_ref, middle_ref, mod_ref = refs[:5]
    both_w = refs[5 : 5 + pieces]
    gs_ref, gl_ref, gm_ref, sums_ref, lift_sums_ref = refs[5 + pieces :]
    grad = g_ref[0].astype(F32)
    scale_b, gate_b = mod_ref[0, 4:5, :], mod_ref[0, 5:6, :]
    grad_second = (gate_b * grad).astype(BF16)
    gs_ref[0] = grad_second
    normed = jnp.zeros_like(grad)
    for c in range(pieces):
        part = both_w[c].shape[2]
        grad_hidden = mm(grad_second, both_w[c][1])
        v = lifted_ref[0, :, c * part : (c + 1) * part].astype(F32)
        square = v * v
        turn = jnp.tanh(GELU_A * v * (1.0 + GELU_B * square))
        slope = 0.5 * (1.0 + turn) + (0.5 * GELU_A) * v * (1.0 - turn * turn) * (
            1.0 + (3.0 * GELU_B) * square
        )
        grad_lifted = (grad_hidden * slope).astype(BF16)
        gl_ref[0, :, c * part : (c + 1) * part] = grad_lifted
        lift_sums_ref[0, c : c + 1, :] = token_sum(grad_lifted.astype(F32))
        normed = normed + mm_nt(grad_lifted, both_w[c][0])
    unit, rate = norm_parts(middle_ref[0])
    gm_ref[0] = grad + norm_back(unit, rate, normed * (1.0 + scale_b))
    sums_ref[0, 0:1, :] = token_sum(normed)
    sums_ref[0, 1:2, :] = token_sum(normed * unit)
    sums_ref[0, 2:3, :] = token_sum(grad * second_ref[0].astype(F32))
    sums_ref[0, 3:4, :] = token_sum(grad_second.astype(F32))


def attend_back_kernel(ways, heads, refs):
    gm_ref, branch_ref, qk_ref, v_ref, x_ref, mod_ref = refs[:6]
    pack_w = refs[6 : 6 + ways]
    gb_ref, gqk_ref, gv_ref, gi_ref, sums_ref, pack_sums_ref = refs[6 + ways :]
    cols = heads * HEAD_DIM
    width = gm_ref.shape[2]
    scale = HEAD_DIM**-0.5
    middle = gm_ref[0]
    scale_a, gate_a = mod_ref[0, 1:2, :], mod_ref[0, 2:3, :]
    grad_branch = (gate_a * middle).astype(BF16)
    gb_ref[0] = grad_branch
    normed = jnp.zeros_like(middle)
    for j in range(ways):
        grad_att = mm(grad_branch, pack_w[j][:width, 2 * cols :]).astype(BF16)
        qk = qk_ref[0, j]
        value = v_ref[0, j]
        grads_q, grads_k, grads_v = [], [], []
        for h in range(heads):
            query, key = head_cols(qk, 0, h), head_cols(qk, cols, h)
            grad_head = head_cols(grad_att, cols, h)
            scores = mm_nt(key, query * jnp.asarray(scale, BF16))
            raised = jnp.exp(scores - jnp.max(scores, axis=0, keepdims=True))
            probs = raised * (1.0 / jnp.sum(raised, axis=0, keepdims=True))
            grads_v.append(mm(probs.astype(BF16), grad_head))
            grad_probs = mm_nt(head_cols(value, 0, h), grad_head)
            total = jnp.sum(grad_probs * probs, axis=0, keepdims=True)
            grad_scores = (probs * (grad_probs - total)).astype(BF16)
            grads_k.append(mm(grad_scores, query) * scale)
            grads_q.append(mm_tn(grad_scores, key) * scale)
        grad_qk = jnp.concatenate(grads_q + grads_k, axis=1).astype(BF16)
        grads_v.append(jnp.zeros((middle.shape[0], cols), F32))
        grad_v = jnp.concatenate(grads_v, axis=1).astype(BF16)
        gqk_ref[0, j] = grad_qk
        gv_ref[0, j] = grad_v
        pack_sums_ref[0, j : j + 1, :] = token_sum(grad_qk.astype(F32))
        pack_sums_ref[0, ways + j : ways + j + 1, :] = token_sum(grad_v.astype(F32))
        normed = normed + mm_nt(grad_qk, pack_w[j][:width, : 2 * cols])
        normed = normed + mm_nt(grad_v, pack_w[j][:width, 2 * cols :])
    unit, rate = norm_parts(x_ref[0].astype(F32))
    gi_ref[0] = (middle + norm_back(unit, rate, normed * (1.0 + scale_a))).astype(BF16)
    sums_ref[0, 0:1, :] = token_sum(normed)
    sums_ref[0, 1:2, :] = token_sum(normed * unit)
    sums_ref[0, 2:3, :] = token_sum(middle * branch_ref[0].astype(F32))
    sums_ref[0, 3:4, :] = token_sum(grad_branch.astype(F32))


def flat_tokens(ref):
    return ref[...].reshape(ref.shape[0] * ref.shape[1], ref.shape[2])


SENT = {1: (1, 3), 2: (2, 3)}
KEPT = {1: (0, 2), 2: (0, 1)}


def lift_weights_kernel(refs):
    nb_ref, gl_ref, gs_ref, hidden_ref = refs[:4]
    outs = {1: refs[4:6], 2: refs[6:8]}
    part = refs[4].shape[2]
    for kind, (left_ref, right_ref) in enumerate(((gs_ref, hidden_ref), (nb_ref, gl_ref))):
        left = flat_tokens(left_ref).T
        for side, first in enumerate((1, 2)):
            for place, blocks in enumerate((SENT[first], KEPT[first])):
                for i, j in enumerate(blocks):
                    c = 2 * j + side
                    right = right_ref[:, :, c * part : (c + 1) * part]
                    right = right.reshape(right.shape[0] * right.shape[1], part)
                    outs[first][place][2 * i + kind] = mm(left, right).astype(BF16)


def attend_weights_kernel(refs):
    na_ref, gqk_ref, gv_ref, gb_ref, att_ref = refs[:5]
    outs = {1: refs[5:7], 2: refs[7:9]}
    latents = na_ref.shape[0]
    left_n = flat_tokens(na_ref).T
    left_b = flat_tokens(gb_ref).T
    over = lambda ref, j: jnp.concatenate([ref[g, j] for g in range(latents)], axis=0)
    for place in range(2):
        for i, j in enumerate((SENT, KEPT)[place][1]):
            outs[1][place][i] = mm(left_n, over(gqk_ref, j)).astype(BF16)
        for i, j in enumerate((SENT, KEPT)[place][2]):
            grad = mm(left_n, over(gv_ref, j)) + mm(left_b, over(att_ref, j))
            outs[2][place][i] = grad.astype(BF16)


def per_latent(shape):
    rank = len(shape)
    return pl.BlockSpec((1,) + tuple(shape[1:]), lambda g: (g,) + (0,) * (rank - 1))


def constant(shape):
    rank = len(shape)
    return pl.BlockSpec(tuple(shape), lambda g: (0,) * rank, pipeline_mode=pl.Buffered(1))


def over_latents(kernel, name, varying, fixed, outs, flops, run=None, others=()):
    flags = [] if run is None else [run]

    def whole(*refs):
        refs = refs[len(flags) :]
        ins, rest = refs[: len(varying)], refs[len(varying) : len(varying) + len(fixed)]
        kernel(ins + rest + refs[-len(outs) :])

    def flagged(*refs):
        flag = refs[0][0]

        @pl.when(flag == 1)
        def _():
            whole(*refs)

        if others:

            @pl.when(flag == 0)
            def _():
                start = 1 + len(varying) + len(fixed)
                for source, target in zip(refs[start : start + len(others)], refs[-len(outs) :]):
                    target[...] = source[...]

    return pl.pallas_call(
        flagged if flags else whole,
        grid=(varying[0].shape[0],),
        in_specs=[pl.BlockSpec(memory_space=pltpu.SMEM)] * len(flags)
        + [per_latent(a.shape) for a in varying]
        + [constant(a.shape) for a in fixed]
        + [per_latent(a.shape) for a in others],
        out_specs=[per_latent(shape) for shape, _ in outs],
        out_shape=[jax.ShapeDtypeStruct(shape, dtype) for shape, dtype in outs],
        compiler_params=pltpu.CompilerParams(vmem_limit_bytes=VMEM_BYTES),
        cost_estimate=pl.CostEstimate(
            flops=flops,
            bytes_accessed=sum(a.size * a.dtype.itemsize for a in varying + fixed)
            + sum(2 * math.prod(shape) for shape, _ in outs),
            transcendentals=0,
        ),
        name=name,
    )(*flags, *varying, *fixed, *others)


def at_once(kernel, name, inputs, out_shapes, flops):
    return pl.pallas_call(
        lambda *refs: kernel(refs),
        in_specs=[pl.BlockSpec(memory_space=pltpu.VMEM)] * len(inputs),
        out_specs=[pl.BlockSpec(memory_space=pltpu.VMEM)] * len(out_shapes),
        out_shape=[jax.ShapeDtypeStruct(shape, BF16) for shape in out_shapes],
        compiler_params=pltpu.CompilerParams(vmem_limit_bytes=VMEM_BYTES),
        cost_estimate=pl.CostEstimate(
            flops=flops,
            bytes_accessed=sum(a.size * a.dtype.itemsize for a in inputs)
            + sum(2 * math.prod(shape) for shape in out_shapes),
            transcendentals=0,
        ),
        name=name,
    )(*inputs)


def attend_forward(tokens_in, mod6, weights, biases):
    pack_w = weights[0]
    b_qk, b_v, b_proj = biases[:3]
    ways, cols = len(pack_w), b_v.shape[1]
    latents, tokens, width = tokens_in.shape
    whole = (latents, tokens, width)
    return over_latents(
        functools.partial(attend_kernel, ways, cols // HEAD_DIM),
        "attend_forward",
        [tokens_in, mod6],
        [b_qk, b_v, b_proj, *pack_w],
        [
            (whole, BF16),
            ((latents, ways, tokens, 2 * cols), BF16),
            ((latents, ways, tokens, cols), BF16),
            ((latents, ways, tokens, 2 * cols), BF16),
            (whole, BF16),
            (whole, F32),
            (whole, BF16),
        ],
        10 * latents * tokens * width * width,
    )


def lift_forward(normed_b, middle, mod6, weights, biases):
    both_w = weights[1]
    b_up, b_down = biases[3:]
    whole = middle.shape
    wide = whole[:2] + (b_up.size,)
    return over_latents(
        functools.partial(lift_kernel, len(both_w)),
        "lift_forward",
        [normed_b, middle, mod6],
        [b_up, b_down, *both_w],
        [(wide, BF16), (wide, BF16), (whole, BF16), (whole, BF16)],
        4 * math.prod(whole) * b_up.size,
    )


def layer_forward(tokens_in, mod6, weights, biases):
    normed_a, qk, value, attended, branch, middle, normed_b = attend_forward(
        tokens_in, mod6, weights, biases
    )
    lifted, hidden, second, output = lift_forward(normed_b, middle, mod6, weights, biases)
    saved_a = (normed_a, qk, value, attended, branch)
    saved_b = (middle, normed_b, lifted, hidden, second)
    return output, saved_a, saved_b


def lift_backward(grad_out, mod6, weights, saved_b, run, others=()):
    both_w = weights[1]
    middle, normed_b, lifted, hidden, second = saved_b
    latents, tokens, width = middle.shape
    grad_second, grad_lifted, grad_middle, sums, lift_sums = over_latents(
        functools.partial(lift_back_kernel, len(both_w)),
        "lift_backward",
        [grad_out, second, lifted, middle, mod6],
        both_w,
        [
            (middle.shape, BF16),
            (lifted.shape, BF16),
            (middle.shape, F32),
            ((latents, 4, width), F32),
            ((latents, len(both_w), both_w[0].shape[2]), F32),
        ],
        4 * middle.size * lifted.shape[2],
        run,
        others,
    )
    outs = (grad_second, grad_lifted, grad_middle, sums, lift_sums)
    return outs, (normed_b, grad_lifted, grad_second, hidden)


def attend_backward(grad_middle, tokens_in, mod6, weights, saved_a, run, others=()):
    pack_w = weights[0]
    normed_a, qk, value, attended, branch = saved_a
    latents, tokens, width = grad_middle.shape
    cols = value.shape[3]
    grad_branch, grad_qk, grad_v, grad_input, sums, pack_sums = over_latents(
        functools.partial(attend_back_kernel, len(pack_w), cols // HEAD_DIM),
        "attend_backward",
        [grad_middle, branch, qk, value, tokens_in, mod6],
        pack_w,
        [
            (grad_middle.shape, BF16),
            (qk.shape, BF16),
            (qk.shape, BF16),
            (grad_middle.shape, BF16),
            ((latents, 4, width), F32),
            ((latents, 2 * len(pack_w), 2 * cols), F32),
        ],
        16 * grad_middle.size * width,
        run,
        others,
    )
    outs = (grad_branch, grad_qk, grad_v, grad_input, sums, pack_sums)
    return outs, (normed_a, grad_qk, grad_v, grad_branch, attended)


def lift_weights(kept):
    normed_b, grad_lifted = kept[:2]
    width, wide = normed_b.shape[2], grad_lifted.shape[2]
    shape = (4, width, wide // 8)
    return at_once(lift_weights_kernel, "lift_weights", kept, [shape] * 4, 4 * normed_b.size * wide)


def attend_weights(kept):
    normed_a, grad_qk = kept[:2]
    shape = (2, normed_a.shape[2], grad_qk.shape[3])
    flops = 6 * normed_a.size * grad_qk.shape[1] * grad_qk.shape[3]
    return at_once(attend_weights_kernel, "attend_weights", kept, [shape] * 4, flops)


def after(value, *others):
    return lax.optimization_barrier((value, others))[0]


def body(
    latents,
    cond,
    cotangent,
    live,
    w_qkv,
    w_proj,
    w_up,
    w_down,
    w_ada,
    bias_qv,
    bias_proj,
    bias_up,
    bias_down,
    bias_ada,
):
    micros, slots, tokens_own, width = latents.shape
    ways = lax.axis_size("tensor")
    dps = lax.axis_size("dp")
    share = micros * slots // ways
    own_t = lax.axis_index("tensor")
    is_first = lax.axis_index("section") == 0
    qkv_cols = w_qkv.shape[3]
    hidden_cols = w_up.shape[2]
    mod_cols = w_ada.shape[2]
    mod_w = w_ada[0]

    source = jnp.where(is_first, latents, cotangent).reshape(ways, share, tokens_own, width)
    tokens_in = jnp.concatenate(send_tensor(source), axis=1)

    half = hidden_cols // 2
    pair_cols = 2 * qkv_cols
    rows = width // dps
    pack_shard = jnp.concatenate(
        [w_qkv[0, :, 0], w_qkv[0, :, 1], w_qkv[0, :, 2], w_proj[0].T], axis=1
    )
    bias_shard = jnp.concatenate(
        [bias_qv[0, 0], bias_qv[0, 1], bias_proj[0], bias_up[0], bias_down[0], bias_ada[0]]
    )
    cuts = [bias_qv.shape[2]] * 2 + [b.shape[1] for b in (bias_proj, bias_up, bias_down, bias_ada)]
    bias_size = sum(cuts)
    latent_count = micros * slots
    act = jax.nn.silu(cond.astype(F32)).astype(BF16).reshape(latent_count, width)
    riders = jnp.concatenate([jnp.pad(bias_shard, (0, width - bias_size))[None], act])
    riders = jnp.pad(riders, ((0, -riders.shape[0] % 16), (0, 0)))
    first_kind = gather_dp(jnp.concatenate([pack_shard, riders]))
    bias_dp = first_kind[:, rows, :bias_size].reshape(-1)
    bias_dp = jnp.pad(bias_dp, (0, -bias_dp.shape[0] % (16 * 2 * pair_cols)))
    pack_own = jnp.concatenate(
        [first_kind[:, :rows].reshape(width, 2 * pair_cols), bias_dp.reshape(-1, 2 * pair_cols)]
    )
    act_all = lax.dynamic_slice_in_dim(
        first_kind[:, rows + 1 : rows + 1 + latent_count],
        lax.axis_index("dp") * rows,
        rows,
        2,
    )
    pack_own = after(pack_own, tokens_in)
    pack_w = [pack_own] + [swap(pack_own, "tensor", j) for j in range(1, ways)]
    second_kind = gather_dp(after(jnp.stack([w_up[0], w_down[0].T]), pack_own))
    mod_terms = dot(after(act_all, pack_own), mod_w, "kgd,dm->kgm")
    mod_terms = mod_terms.reshape(dps * ways, share, mod_cols)
    mod_block = lax.all_to_all(mod_terms, ("dp", "tensor"), 0, 0)
    mod_block = jnp.sum(mod_block.reshape(dps, ways, share, mod_cols), axis=0)
    both_own = jnp.transpose(second_kind, (1, 0, 2, 3)).reshape(2, width, hidden_cols)

    bias_rel = jnp.stack([part[width:].reshape(-1)[: dps * bias_size] for part in pack_w])
    bias_all = ordered(bias_rel).reshape(ways, dps, bias_size)
    bias_all = jnp.transpose(bias_all, (1, 0, 2)).astype(F32)
    full, start = [], 0
    for cut in cuts:
        full.append(bias_all[:, :, start : start + cut].reshape(-1))
        start += cut
    full_q, full_v, full_proj, full_up, full_down, full_ada = full
    by_xor = lambda vector: ordered(vector.reshape(ways, -1)).reshape(-1)
    bias_qk = by_xor(full_q).reshape(ways, -1)
    bias_qk = jnp.concatenate([bias_qk, jnp.zeros_like(bias_qk)], axis=1)
    biases = (
        bias_qk,
        by_xor(full_v).reshape(ways, -1),
        full_proj[None],
        by_xor(full_up).reshape(2 * ways, -1),
        full_down[None],
    )

    modulate = jnp.transpose(mod_block, (1, 0, 2)).reshape(share, ways * mod_cols) + full_ada
    mod6 = modulate.reshape(share, 6, width)

    both_a = spread_tensor(after(both_own[:, :, :half], pack_w), 1, 2)
    both_b = spread_tensor(after(both_own[:, :, half:], pack_w), 2, 1)
    weights = (pack_w, [piece for pair in zip(both_a, both_b) for piece in pair])

    slot_mask = (lax.broadcasted_iota(jnp.int32, (micros, slots), 1) < live).astype(F32)
    own_mask = pick(slot_mask.reshape(ways, share), own_t)

    on_first = jnp.where(is_first, 1, 0).astype(jnp.int32).reshape(1)

    def handed_back(whole):
        split = jnp.transpose(whole.reshape(share, ways, tokens_own, width), (1, 0, 2, 3))
        arrivals = [split[0]] + [swap(split[j], "tensor", j) for j in range(1, ways)]
        return ordered(jnp.stack(arrivals)).reshape(latents.shape)

    output_first = layer_forward(tokens_in, mod6, weights, biases)[0]
    arrived = lax.ppermute(output_first, "section", [(0, 1)])
    incoming = jnp.where(is_first, tokens_in, arrived)
    output, saved_a, saved_b = layer_forward(incoming, mod6, weights, biases)

    grad_out = tokens_in * own_mask[:, None, None].astype(BF16)
    lift_1, _ = lift_backward(grad_out, mod6, weights, saved_b, 1 - on_first)
    layer_out = handed_back(output)
    grad_middle, layer_out = lax.optimization_barrier((lift_1[2], layer_out))
    attend_1, _ = attend_backward(grad_middle, incoming, mod6, weights, saved_a, 1 - on_first)
    back = lax.ppermute(attend_1[3], "section", [(1, 0)])

    lift_outs, kept_b = lift_backward(back, mod6, weights, saved_b, on_first, lift_1)
    lift_slabs = lift_weights(kept_b)
    attend_outs, kept_a = attend_backward(
        after(lift_outs[2], lift_slabs), incoming, mod6, weights, saved_a, on_first, attend_1
    )
    sums_b = lift_outs[3:]
    grad_input, sums_a = attend_outs[3], attend_outs[4:]
    attend_slabs = attend_weights(kept_a)
    near_a, onward_a = first_hop(*lift_slabs[:2], 1)
    near_b, onward_b = first_hop(*lift_slabs[2:], 2)
    sums_a, sums_b = after((sums_a, sums_b), onward_a, onward_b, attend_slabs)

    grad_mod = jnp.concatenate([sums_a[0][:, :3], sums_b[0][:, :3]], axis=1)
    grad_mod = grad_mod.reshape(share, 6 * width).astype(BF16)

    pack_sums = jnp.sum(sums_a[1], axis=0)
    parts = [
        by_xor(pack_sums[:ways, :qkv_cols].reshape(-1)),
        by_xor(pack_sums[ways:, :qkv_cols].reshape(-1)),
        jnp.sum(sums_a[0][:, 3], axis=0),
        by_xor(jnp.sum(sums_b[1], axis=0).reshape(-1)),
        jnp.sum(sums_b[0][:, 3], axis=0),
        jnp.sum(grad_mod.astype(F32), axis=0),
    ]
    bias_terms = jnp.concatenate([part.reshape(dps, ways, -1) for part in parts], axis=2)
    bias_terms = jnp.transpose(bias_terms, (1, 0, 2)).reshape(ways, -1)
    grad_groups = jnp.transpose(grad_mod.reshape(share, ways, mod_cols), (1, 0, 2))
    grad_groups = grad_groups.reshape(ways, -1).astype(F32)
    mod_size = grad_groups.shape[1]
    arrivals = jnp.concatenate([grad_groups, bias_terms], axis=1)
    arrivals = lax.all_to_all(arrivals, "tensor", 0, 0)
    grad_block = arrivals[:, :mod_size].reshape(latent_count, mod_cols)
    bias_terms = jnp.sum(arrivals[:, mod_size:], axis=0).reshape(dps, bias_size)

    grad_block = jnp.broadcast_to(grad_block.reshape(1, -1), (dps, grad_block.size))
    shared = lax.all_to_all(jnp.concatenate([grad_block, bias_terms], axis=1), "dp", 0, 0)
    grad_all = shared[:, : -bias_size].reshape(dps, latent_count, mod_cols).astype(BF16)
    bias_out = jnp.sum(shared[:, -bias_size:], axis=0)

    lift_a = second_hop(lift_slabs[1], near_a, after(onward_a, arrivals), 2)
    lift_b = second_hop(lift_slabs[3], near_b, after(onward_b, arrivals), 1)
    near_a, onward_a = first_hop(after(attend_slabs[0], arrivals), attend_slabs[1], 1)
    near_b, onward_b = first_hop(after(attend_slabs[2], arrivals), attend_slabs[3], 2)
    out_lift = scatter_rows([lift_a, lift_b])
    sum_qk = second_hop(attend_slabs[1], near_a, onward_a, 2)
    sum_vp = second_hop(attend_slabs[3], near_b, onward_b, 1)
    out_attend = scatter_rows([sum_qk, sum_vp])
    shard_down = jnp.concatenate([out_lift[0], out_lift[2]], axis=1).T
    shard_up = jnp.concatenate([out_lift[1], out_lift[3]], axis=1)
    shard_qkv = jnp.concatenate([out_attend[0], out_attend[1][:, :qkv_cols]], axis=1)
    shard_qkv = shard_qkv.reshape(-1, 3, qkv_cols)
    shard_proj = out_attend[1][:, qkv_cols:].T

    shard_ada = dot(act_all, grad_all, "kgd,kgm->dm")
    ctx_terms = dot(after(grad_all, out_lift), mod_w, "kgm,dm->kgd").astype(BF16)
    ctx_terms = lax.all_to_all(ctx_terms, "dp", 0, 0)
    ctx = jnp.transpose(ctx_terms, (1, 0, 2)).reshape(latent_count, width)
    ctx, grad_input = after((ctx, grad_input), sum_qk, sum_vp)
    for axis, step in (("tensor", 1), ("tensor", 2), ("section", 1)):
        if axis == "section":
            ctx = after(ctx, out_attend, out_lift)
        ctx = (ctx.astype(F32) + swap(ctx, axis, step).astype(F32)).astype(BF16)
    silu_back = jax.vjp(jax.nn.silu, cond.astype(F32))[1]
    cond_grad = silu_back(ctx.astype(F32).reshape(cond.shape))[0].astype(BF16)
    bias_pieces, start = [], 0
    for cut in cuts:
        bias_pieces.append(bias_out[start : start + cut])
        start += cut

    input_grad = handed_back(grad_input)
    return (
        layer_out[None],
        input_grad[None],
        cond_grad,
        shard_qkv[None],
        shard_proj[None],
        shard_up[None],
        shard_down[None],
        shard_ada[None],
        jnp.stack(bias_pieces[:2])[None],
        bias_pieces[2][None],
        bias_pieces[3][None],
        bias_pieces[4][None],
        bias_pieces[5][None],
    )


def solution(mesh):
    both = ("dp", "tensor")
    return jax.shard_map(
        body,
        mesh=mesh,
        in_specs=(
            P(None, "dp", "tensor", None),
            P(None, "dp", None),
            P(None, "dp", "tensor", None),
            P(None, "dp"),
            P("section", "dp", None, "tensor"),
            P("section", "tensor", "dp"),
            P("section", "dp", "tensor"),
            P("section", "tensor", "dp"),
            P("section", "dp", "tensor"),
            P("section", None, both),
            P("section", both),
            P("section", both),
            P("section", both),
            P("section", both),
        ),
        out_specs=(
            P("section", None, "dp", "tensor", None),
            P("section", None, "dp", "tensor", None),
            P(None, "dp", None),
            P("section", "dp", None, "tensor"),
            P("section", "tensor", "dp"),
            P("section", "dp", "tensor"),
            P("section", "tensor", "dp"),
            P("section", "dp", "tensor"),
            P("section", None, both),
            P("section", both),
            P("section", both),
            P("section", both),
            P("section", both),
        ),
        check_vma=False,
    )
```
